32 devices in a mesh: grp: 4 (over x, core), dev: 8 (over z, y).
Axes of the slice: x: 2, y: 2, z: 4, core: 2. Of those that a mesh axis runs over, the one named last changes fastest.
Arguments:
- views_a: bfloat16 [8192, 256], P(('grp', 'dev')), may hold values from -6 to 6
- views_b: bfloat16 [8192, 256], P(('grp', 'dev')), may hold values from -6 to 6
- positives: int32 [8192], P(('grp', 'dev')), may hold values from 0 to 8191, as said below
- plan: int32 [2, 4], replicated, may hold values from 0 to 3, as said below
Outputs:
- grad_a: float32 [8192, 256], P(('grp', 'dev'))
- grad_b: float32 [8192, 256], P(('grp', 'dev'))
The draws below stay inside these ranges and needn't reach their ends.
Inputs may be any that keep to these rules, and one draw needn't show every extreme that they name: Row r holds a round of one round-robin over the 4 groups: plan[r, plan[r, g]] == g and plan[r, g] != g; no two rows pair the same two groups. positives[i] is i itself or a view of a group that plan pairs with the group of view i in some row.
All inputs are finite; a program needn't handle non-finite values.
Results may differ from the reference program's by a relative error of at most 0.00057.
Values may be sent and summed in bfloat16 or wider, within the bound.
A program may use at most 128 MiB of HBM per device.

```python
import math
import jax
import jax.numpy as jnp
from jax import lax

D = 256
ROWS_DEV = 256
ROUNDS = 2
GROUPS = 4
GROUP_ROWS = 2048
VIEWS = 8192


def round_table(key):
    perm_key, pick_key = jax.random.split(key)
    players = GROUPS - 1
    labels = jax.random.permutation(perm_key, GROUPS).astype(jnp.int32)
    chosen = jax.random.permutation(pick_key, players).astype(jnp.int32)
    seats = jnp.arange(GROUPS, dtype=jnp.int32)
    table_rows = []
    for slot in range(ROUNDS):
        picked = chosen[slot]
        mates = (2 * picked - seats) % players
        mates = jnp.where(mates == seats, players, mates)
        mates = jnp.where(seats == players, picked, mates)
        table_rows.append(jnp.zeros((GROUPS,), jnp.int32).at[labels].set(labels[mates]))
    return jnp.stack(table_rows).astype(jnp.int32)


def draw_plan(key, part):
    return round_table(key)


def draw_positives(key, part):
    table = round_table(key)
    key = jax.random.fold_in(key, 7)
    which_key, row_key = jax.random.split(key)
    views = jnp.arange(VIEWS, dtype=jnp.int32)
    group = views // GROUP_ROWS
    which = jax.random.randint(which_key, (VIEWS,), 0, ROUNDS + 1).astype(jnp.int32)
    which = which.at[VIEWS - 1].set(0).at[0].set(0)
    partner = table[jnp.clip(which - 1, 0, ROUNDS - 1), group]
    local = jax.random.randint(row_key, (VIEWS,), 0, GROUP_ROWS).astype(jnp.int32)
    return jnp.where(which == 0, views, partner * GROUP_ROWS + local).astype(jnp.int32)


def shard_levels(stream_key, dims, pieces, smallest, top_value):
    level, own = 1.0, jax.random.fold_in(stream_key, 6)
    for position, blocks in pieces:
        heights = jnp.exp(jax.random.uniform(jax.random.fold_in(own, position), (blocks,), jnp.float32, smallest / len(pieces), top_value / len(pieces)))
        level = level * jnp.repeat(heights, dims[position] // blocks).reshape([-1 if axis == position else 1 for axis in range(len(dims))])
    return level


def noise(own_key, shape, spread, reach, shards=(), held_as=jnp.bfloat16):
    factor_of = shard_levels(own_key, shape, shards, -0.22, 0.18) if shards else 1.0
    drawn = jax.random.normal(own_key, shape, jnp.float32) * spread * factor_of
    return jnp.minimum(jnp.maximum(drawn, -reach), reach).astype(held_as)


def setup_inputs(seed: int = 0) -> dict:
    key_of = jax.random.split(jax.random.key(seed), 5)
    views_a = noise(key_of[0], (VIEWS, D), 1.0, 6.0, ((0, 32),))
    views_b = noise(key_of[1], (VIEWS, D), 1.0, 6.0, ((0, 32),))
    positives = draw_positives(jax.random.fold_in(key_of[4], 71), 0)
    plan = draw_plan(jax.random.fold_in(key_of[4], 71), 0)
    return dict(views_a=views_a, views_b=views_b, positives=positives, plan=plan)


logit_scale = 2.0
logit_bias = -6.0

def reference(views_a, views_b, positives, plan):
    factor = logit_scale / math.sqrt(D)
    blocks = VIEWS // ROWS_DEV

    def step(grad_b, index):
        start = (index * ROWS_DEV).astype(jnp.int32)
        group = (start // GROUP_ROWS).astype(jnp.int32)
        queries = lax.dynamic_slice_in_dim(views_a, start, ROWS_DEV, 0)
        labels = lax.dynamic_slice_in_dim(positives, start, ROWS_DEV, 0)
        owners = jnp.concatenate([group[None], plan[:, group].astype(jnp.int32)])
        grad_block = jnp.zeros((ROWS_DEV, D), jnp.float32)
        for slot in range(ROUNDS + 1):
            first = (owners[slot] * GROUP_ROWS).astype(jnp.int32)
            keys = lax.dynamic_slice_in_dim(views_b, first, GROUP_ROWS, 0)
            logits = jnp.dot(queries, keys.T, preferred_element_type=jnp.float32) * factor + logit_bias
            columns = first + jnp.arange(GROUP_ROWS, dtype=jnp.int32)
            hit = (labels[:, None] == columns[None, :]).astype(jnp.float32)
            weights = (jax.nn.sigmoid(logits) - hit).astype(jnp.bfloat16)
            grad_block = grad_block + jnp.dot(weights, keys, preferred_element_type=jnp.float32)
            part = jnp.dot(weights.T, queries, preferred_element_type=jnp.float32)
            current = lax.dynamic_slice_in_dim(grad_b, first, GROUP_ROWS, 0)
            grad_b = lax.dynamic_update_slice_in_dim(grad_b, current + part, first, 0)
        return (grad_b, grad_block)
    grad_b, grad_blocks = lax.scan(step, jnp.zeros((VIEWS, D), jnp.float32), jnp.arange(blocks, dtype=jnp.int32))
    return (grad_blocks.reshape(VIEWS, D) * factor, grad_b * factor)
```

```python
import functools
import math

import jax
import jax.numpy as jnp
from jax import lax
from jax.experimental import pallas as pl
from jax.experimental.pallas import tpu as pltpu
from jax.sharding import PartitionSpec as P

logit_scale = 2.0
logit_bias = -6.0

MESH = pl.DeviceIdType.MESH
RIGHT, LEFT, CROSS, SIBLING = range(4)
EXTRA = 16


def dot_rows(left, right):
    return lax.dot_general(left, right, (((1,), (1,)), ((), ())), preferred_element_type=jnp.float32)


def kernel(
    n, factor, a_in, b_in, labels_in, plan, out_a, out_b,
    held_a, held_b, scaled_a, scaled_b, offsets, recv_a, recv_b, send_a, send_b,
):
    rows, width = a_in.shape
    half = n // 2
    group, member = lax.axis_index("grp"), lax.axis_index("dev")
    x, core = lax.div(group, 2), lax.rem(group, 2)
    groups = (group, (1 - x) * 2 + core, x * 2 + 1 - core, (1 - x) * 2 + 1 - core)

    odd, pair = lax.rem(member, 2), lax.div(member, 2)
    place = (1 - odd) * pair + odd * (n - 1 - pair)

    def member_at(spot):
        back = lax.div(spot, half)
        return (1 - back) * 2 * spot + back * (2 * (n - 1 - spot) + 1)

    targets = (
        (group, member_at(lax.rem(place + 1, n))),
        (group, member_at(lax.rem(place + n - 1, n))),
        (groups[1], member),
        (groups[2], member),
    )

    def behind(step):
        return lax.rem(place + n - step, n)

    def ahead(step):
        return lax.rem(place + step, n)

    def copy(side, q, spot, kind):
        held, recv, send = ((held_a, recv_a, send_a), (held_b, recv_b, send_b))[side]
        slot = groups[q] * n + spot
        return pltpu.make_async_remote_copy(
            src_ref=held.at[slot],
            dst_ref=held.at[slot],
            send_sem=send.at[kind, (q % 2) * n + spot],
            recv_sem=recv.at[slot],
            device_id=targets[kind],
            device_id_type=MESH,
        )

    def arrived(side, q, spot):
        copy(side, q, spot, SIBLING).wait_recv()

    def start(side, q, spot, kind):
        copy(side, q, spot, kind).start()

    def sent(side, q, spot, kind):
        copy(side, q, spot, kind).wait_send()

    def send_b_behind(step, act, first=None):
        @pl.when(step < half)
        def _():
            spot = behind(step)
            if first is not None:
                first(1, 0, spot)

            @pl.when(step < half - 1)
            def _():
                act(1, 0, spot, RIGHT)

            act(1, 0, spot, CROSS)
            act(1, 0, spot, SIBLING)

    def send_b_ahead(step, act, first=None):
        @pl.when(step <= half)
        def _():
            spot = ahead(step)
            if first is not None:
                first(1, 0, spot)

            @pl.when(step < half)
            def _():
                act(1, 0, spot, LEFT)

            act(1, 0, spot, CROSS)
            act(1, 0, spot, SIBLING)

    def send_a_behind(q, step, act, first=None):
        @pl.when(step <= half)
        def _():
            spot = behind(step)
            if first is not None:
                first(0, q, spot)

            @pl.when(step < half)
            def _():
                act(0, q, spot, RIGHT)

            act(0, q, spot, SIBLING)

    def send_a_ahead(q, step, act, first=None):
        @pl.when(step < half)
        def _():
            spot = ahead(step)
            if first is not None:
                first(0, q, spot)

            @pl.when(step < half - 1)
            def _():
                act(0, q, spot, LEFT)

            act(0, q, spot, SIBLING)

    def send_own(act):
        act(0, 0, place, CROSS)
        act(0, 0, place, RIGHT)
        act(1, 0, place, LEFT)
        if half > 1:
            act(1, 0, place, RIGHT)
            act(0, 0, place, LEFT)
        act(1, 0, place, CROSS)
        act(0, 0, place, SIBLING)
        act(1, 0, place, SIBLING)

    def send_crossed(act):
        act(0, 1, place, RIGHT)
        if half > 1:
            act(0, 1, place, LEFT)
        act(0, 1, place, SIBLING)

    barrier = pltpu.get_barrier_semaphore()
    for target in targets:
        pl.semaphore_signal(barrier, inc=1, device_id=target, device_id_type=MESH)

    mine = group * n + place
    labels = labels_in[...]
    high = lax.shift_right_logical(labels, 8).astype(jnp.float32)
    low = jnp.bitwise_and(labels, 255).astype(jnp.float32)
    line = lax.broadcasted_iota(jnp.int32, (EXTRA, rows), 0)
    coded = jnp.where(line == 0, high, jnp.where(line == 1, low, 0.0))
    held_a[mine, 0:rows, :] = a_in[...]
    held_a[mine, rows : rows + EXTRA, :] = coded.astype(jnp.bfloat16)
    held_b[mine] = b_in[...]
    pl.semaphore_wait(barrier, 4)
    send_own(start)

    scaled_a[...] = (a_in[...].astype(jnp.float32) * (0.5 * factor)).astype(jnp.bfloat16)
    scaled_b[...] = (b_in[...].astype(jnp.float32) * (0.5 * factor)).astype(jnp.bfloat16)
    column = lax.broadcasted_iota(jnp.int32, (rows, rows), 1).astype(jnp.float32)
    offsets[...] = (
        jnp.transpose(jnp.broadcast_to(labels.astype(jnp.float32), (rows, rows))) - column
    )
    out_a[...] = jnp.zeros_like(out_a)
    out_b[...] = jnp.zeros_like(out_b)
    own_first = ((group * n + member) * rows).astype(jnp.float32)

    arrived(0, 1, place)
    send_crossed(start)

    def bias_of(other):
        inside = other == group
        for slot in range(plan.shape[0]):
            inside = jnp.logical_or(inside, other == plan[slot, group])
        return jnp.where(inside, 0.5 * logit_bias, -1e30).astype(jnp.float32)

    def work(q, spot):
        slot = groups[q] * n + spot
        bias = bias_of(groups[q])
        first = (((groups[q] * n) + member_at(spot)) * rows).astype(jnp.float32)
        keys = held_b[slot]
        queries = held_a[slot, 0:rows, :]
        code = held_a[slot, rows : rows + EXTRA, :].astype(jnp.float32)
        found = code[0:1] * 256.0 + code[1:2] - own_first
        half_a = jnp.tanh(dot_rows(scaled_a[...], keys) + bias)
        weights = 0.5 * half_a + jnp.where(offsets[...] == first, -0.5, 0.5)
        out_a[...] += jnp.dot(
            weights.astype(jnp.bfloat16), keys, preferred_element_type=jnp.float32
        )
        half_b = jnp.tanh(dot_rows(scaled_b[...], queries) + bias)
        row = lax.broadcasted_iota(jnp.int32, (rows, rows), 0).astype(jnp.float32)
        weights = 0.5 * half_b + jnp.where(found == row, -0.5, 0.5)
        out_b[...] += jnp.dot(
            weights.astype(jnp.bfloat16), queries, preferred_element_type=jnp.float32
        )

    def step_body(step, carry):
        last = step - 1
        count = jnp.where(jnp.logical_or(last == 0, last == half), 1, 2)

        def spot_of(index):
            return lax.rem(place + n + (2 * index - 1) * last, n)

        def work_on(q):
            def body(index, carry):
                work(q, spot_of(index))
                return carry

            lax.fori_loop(0, count, body, 0)

        def receive(q):
            def body(index, carry):
                spot = spot_of(index)
                if q != 1:
                    arrived(0, q, spot)
                arrived(1, q, spot)
                if q == 1:
                    start(1, 1, spot, SIBLING)
                return carry

            lax.fori_loop(0, count, body, 0)

        work_on(0)
        receive(1)
        work_on(1)
        receive(2)
        work_on(2)
        send_b_behind(step, start, arrived)
        send_b_ahead(step, start, arrived)
        receive(3)
        work_on(3)
        for q in range(2):
            send_a_behind(q, step, start, arrived)
            send_a_ahead(q, step, start, arrived)
        return carry

    lax.fori_loop(1, half + 2, step_body, 0)

    out_a[...] = out_a[...] * factor
    out_b[...] = out_b[...] * factor

    send_own(sent)
    send_crossed(sent)

    def drain_body(step, carry):
        send_b_behind(step, sent)
        send_b_ahead(step, sent)
        for q in range(2):
            send_a_behind(q, step, sent)
            send_a_ahead(q, step, sent)
        return carry

    lax.fori_loop(1, half + 1, drain_body, 0)

    def drain_crossed(spot, carry):
        sent(1, 1, spot, SIBLING)
        return carry

    lax.fori_loop(0, n, drain_crossed, 0)


def shards(views_a, views_b, positives, plan):
    rows, width = views_a.shape
    n = lax.axis_size("dev")
    slots = lax.axis_size("grp") * n
    factor = logit_scale / math.sqrt(width)
    held = slots * (2 * rows + EXTRA) * width * 2
    vmem = pl.BlockSpec(memory_space=pltpu.VMEM)
    out = jax.ShapeDtypeStruct((rows, width), jnp.float32)
    return pl.pallas_call(
        functools.partial(kernel, n, factor),
        out_shape=(out, out),
        in_specs=[vmem, vmem, vmem, pl.BlockSpec(memory_space=pltpu.SMEM)],
        out_specs=(vmem, vmem),
        scratch_shapes=[
            pltpu.VMEM((slots, rows + EXTRA, width), jnp.bfloat16),
            pltpu.VMEM((slots, rows, width), jnp.bfloat16),
            pltpu.VMEM((rows, width), jnp.bfloat16),
            pltpu.VMEM((rows, width), jnp.bfloat16),
            pltpu.VMEM((rows, rows), jnp.float32),
            pltpu.SemaphoreType.DMA((slots,)),
            pltpu.SemaphoreType.DMA((slots,)),
            pltpu.SemaphoreType.DMA((4, slots // 2)),
            pltpu.SemaphoreType.DMA((4, slots // 2)),
        ],
        compiler_params=pltpu.CompilerParams(
            collective_id=0, has_side_effects=True, vmem_limit_bytes=held + (10 << 20)
        ),
        cost_estimate=pl.CostEstimate(
            flops=8 * slots * rows * rows * width,
            bytes_accessed=4 * rows * width * 4,
            transcendentals=2 * slots * rows * rows,
        ),
    )(views_a, views_b, positives.reshape(1, rows), plan)


def solution(mesh):
    placed = (P(("grp", "dev"), None), P(("grp", "dev"), None), P(("grp", "dev")), P())
    return jax.shard_map(
        shards,
        mesh=mesh,
        in_specs=placed,
        out_specs=(P(("grp", "dev"), None), P(("grp", "dev"), None)),
        check_vma=False,
    )
```

```python
import functools
import math

import jax
import jax.numpy as jnp
from jax import lax
from jax.experimental import pallas as pl
from jax.experimental.pallas import tpu as pltpu
from jax.sharding import PartitionSpec as P

logit_scale = 2.0
logit_bias = -6.0

MESH = pl.DeviceIdType.MESH
RIGHT, LEFT, CROSS, SIBLING = range(4)
EXTRA = 16


def dot_rows(left, right):
    return lax.dot_general(left, right, (((1,), (1,)), ((), ())), preferred_element_type=jnp.float32)


def kernel(
    n, factor, a_in, b_in, labels_in, plan_in, out_a, out_b,
    held_a, held_b, scaled_a, scaled_b, offsets, labels_held, plan,
    own_sems, recv_a, recv_b, send_a, send_b,
):
    rows, width = a_in.shape
    half = n // 2
    group, member = lax.axis_index("grp"), lax.axis_index("dev")
    x, core = lax.div(group, 2), lax.rem(group, 2)
    groups = (group, (1 - x) * 2 + core, x * 2 + 1 - core, (1 - x) * 2 + 1 - core)

    odd, pair = lax.rem(member, 2), lax.div(member, 2)
    place = (1 - odd) * pair + odd * (n - 1 - pair)

    def member_at(spot):
        back = lax.div(spot, half)
        return (1 - back) * 2 * spot + back * (2 * (n - 1 - spot) + 1)

    targets = (
        (group, member_at(lax.rem(place + 1, n))),
        (group, member_at(lax.rem(place + n - 1, n))),
        (groups[1], member),
        (groups[2], member),
    )

    def behind(step):
        return lax.rem(place + n - step, n)

    def ahead(step):
        return lax.rem(place + step, n)

    def copy(side, q, spot, kind):
        held, recv, send = ((held_a, recv_a, send_a), (held_b, recv_b, send_b))[side]
        slot = groups[q] * n + spot
        return pltpu.make_async_remote_copy(
            src_ref=held.at[slot],
            dst_ref=held.at[slot],
            send_sem=send.at[kind, (q % 2) * n + spot],
            recv_sem=recv.at[slot],
            device_id=targets[kind],
            device_id_type=MESH,
        )

    def arrived(side, q, spot):
        copy(side, q, spot, SIBLING).wait_recv()

    def start(side, q, spot, kind):
        copy(side, q, spot, kind).start()

    def sent(side, q, spot, kind):
        copy(side, q, spot, kind).wait_send()

    def send_b_behind(step, act, first=None):
        @pl.when(step < half)
        def _():
            spot = behind(step)
            if first is not None:
                first(1, 0, spot)

            @pl.when(step < half - 1)
            def _():
                act(1, 0, spot, RIGHT)

            act(1, 0, spot, CROSS)
            act(1, 0, spot, SIBLING)

    def send_b_ahead(step, act, first=None):
        @pl.when(step <= half)
        def _():
            spot = ahead(step)
            if first is not None:
                first(1, 0, spot)

            @pl.when(step < half)
            def _():
                act(1, 0, spot, LEFT)

            act(1, 0, spot, CROSS)
            act(1, 0, spot, SIBLING)

    def send_a_behind(q, step, act, first=None):
        farthest = half - q

        @pl.when(step <= farthest)
        def _():
            spot = behind(step)
            if first is not None:
                first(0, q, spot)

            @pl.when(step < farthest)
            def _():
                act(0, q, spot, RIGHT)

            if q == 0:

                @pl.when(step == half)
                def _():
                    act(0, q, spot, CROSS)

            act(0, q, spot, SIBLING)

    def send_a_ahead(q, step, act, first=None):
        @pl.when(step < half)
        def _():
            spot = ahead(step)
            if first is not None:
                first(0, q, spot)

            @pl.when(step < half - 1)
            def _():
                act(0, q, spot, LEFT)

            act(0, q, spot, SIBLING)

    def send_own(act):
        act(0, 0, place, CROSS)
        act(0, 0, place, RIGHT)
        act(1, 0, place, LEFT)
        if half > 1:
            act(1, 0, place, RIGHT)
            act(0, 0, place, LEFT)
        act(1, 0, place, CROSS)
        act(0, 0, place, SIBLING)
        act(1, 0, place, SIBLING)

    def send_crossed(act):
        if half > 1:
            act(0, 1, place, RIGHT)
            act(0, 1, place, LEFT)
        act(0, 1, place, SIBLING)

    barrier = pltpu.get_barrier_semaphore()
    for target in targets:
        pl.semaphore_signal(barrier, inc=1, device_id=target, device_id_type=MESH)

    mine = group * n + place
    loads = (
        pltpu.make_async_copy(a_in, held_a.at[mine, 0:rows, :], own_sems.at[0]),
        pltpu.make_async_copy(b_in, held_b.at[mine], own_sems.at[1]),
        pltpu.make_async_copy(labels_in, labels_held, own_sems.at[2]),
        pltpu.make_async_copy(plan_in, plan, own_sems.at[3]),
    )
    for load in loads:
        load.start()
    for load in loads:
        load.wait()
    labels = labels_held[...]
    high = lax.shift_right_logical(labels, 8).astype(jnp.float32)
    low = jnp.bitwise_and(labels, 255).astype(jnp.float32)
    line = lax.broadcasted_iota(jnp.int32, (EXTRA, rows), 0)
    coded = jnp.where(line == 0, high, jnp.where(line == 1, low, 0.0))
    held_a[mine, rows : rows + EXTRA, :] = coded.astype(jnp.bfloat16)
    pl.semaphore_wait(barrier, 4)
    send_own(start)

    own_a, own_b = held_a[mine, 0:rows, :], held_b[mine]
    scaled_a[...] = (own_a.astype(jnp.float32) * (0.5 * factor)).astype(jnp.bfloat16)
    scaled_b[...] = (own_b.astype(jnp.float32) * (0.5 * factor)).astype(jnp.bfloat16)
    column = lax.broadcasted_iota(jnp.int32, (rows, rows), 1).astype(jnp.float32)
    offsets[...] = (
        jnp.transpose(jnp.broadcast_to(labels.astype(jnp.float32), (rows, rows))) - column
    )
    out_a[...] = jnp.zeros_like(out_a)
    out_b[...] = jnp.zeros_like(out_b)
    own_first = ((group * n + member) * rows).astype(jnp.float32)

    arrived(0, 1, place)
    send_crossed(start)

    def bias_of(other):
        inside = other == group
        for slot in range(plan.shape[0]):
            inside = jnp.logical_or(inside, other == plan[slot, group])
        return jnp.where(inside, 0.5 * logit_bias, -1e30).astype(jnp.float32)

    def work(q, spot):
        slot = groups[q] * n + spot
        bias = bias_of(groups[q])
        first = (((groups[q] * n) + member_at(spot)) * rows).astype(jnp.float32)
        keys = held_b[slot]
        queries = held_a[slot, 0:rows, :]
        code = held_a[slot, rows : rows + EXTRA, :].astype(jnp.float32)
        found = code[0:1] * 256.0 + code[1:2] - own_first
        half_a = jnp.tanh(dot_rows(scaled_a[...], keys) + bias)
        weights = 0.5 * half_a + jnp.where(offsets[...] == first, -0.5, 0.5)
        out_a[...] += jnp.dot(
            weights.astype(jnp.bfloat16), keys, preferred_element_type=jnp.float32
        )
        half_b = jnp.tanh(dot_rows(scaled_b[...], queries) + bias)
        row = lax.broadcasted_iota(jnp.int32, (rows, rows), 0).astype(jnp.float32)
        weights = 0.5 * half_b + jnp.where(found == row, -0.5, 0.5)
        out_b[...] += jnp.dot(
            weights.astype(jnp.bfloat16), queries, preferred_element_type=jnp.float32
        )

    def step_body(step, carry):
        last = step - 1
        count = jnp.where(jnp.logical_or(last == 0, last == half), 1, 2)

        def spot_of(index):
            return lax.rem(place + n + (2 * index - 1) * last, n)

        def work_on(q):
            def body(index, carry):
                work(q, spot_of(index))
                return carry

            lax.fori_loop(0, count, body, 0)

        def receive(q):
            def body(index, carry):
                spot = spot_of(index)
                if q == 1:

                    @pl.when(last == half)
                    def _():
                        arrived(0, 1, spot)
                        start(0, 1, spot, SIBLING)

                else:
                    arrived(0, q, spot)
                arrived(1, q, spot)
                if q == 1:
                    start(1, 1, spot, SIBLING)
                return carry

            lax.fori_loop(0, count, body, 0)

        send_b_behind(step, start, arrived)
        send_b_ahead(step, start, arrived)
        receive(1)
        work_on(0)
        send_a_behind(0, step, start, arrived)
        send_a_ahead(0, step, start, arrived)
        receive(2)
        work_on(2)
        send_a_behind(1, step, start, arrived)
        send_a_ahead(1, step, start, arrived)
        work_on(1)
        receive(3)
        work_on(3)
        return carry

    lax.fori_loop(1, half + 2, step_body, 0)

    out_a[...] = out_a[...] * factor
    out_b[...] = out_b[...] * factor

    send_own(sent)
    send_crossed(sent)

    def drain_body(step, carry):
        send_b_behind(step, sent)
        send_b_ahead(step, sent)
        for q in range(2):
            send_a_behind(q, step, sent)
            send_a_ahead(q, step, sent)
        return carry

    lax.fori_loop(1, half + 1, drain_body, 0)

    def drain_crossed(spot, carry):
        sent(1, 1, spot, SIBLING)
        return carry

    lax.fori_loop(0, n, drain_crossed, 0)
    sent(0, 1, ahead(half), SIBLING)


def shards(views_a, views_b, positives, plan):
    rows, width = views_a.shape
    n = lax.axis_size("dev")
    slots = lax.axis_size("grp") * n
    factor = logit_scale / math.sqrt(width)
    held = slots * (2 * rows + EXTRA) * width * 2
    vmem = pl.BlockSpec(memory_space=pltpu.VMEM)
    out = jax.ShapeDtypeStruct((rows, width), jnp.float32)
    return pl.pallas_call(
        functools.partial(kernel, n, factor),
        out_shape=(out, out),
        in_specs=[pl.BlockSpec(memory_space=pltpu.HBM)] * 4,
        out_specs=(vmem, vmem),
        scratch_shapes=[
            pltpu.VMEM((slots, rows + EXTRA, width), jnp.bfloat16),
            pltpu.VMEM((slots, rows, width), jnp.bfloat16),
            pltpu.VMEM((rows, width), jnp.bfloat16),
            pltpu.VMEM((rows, width), jnp.bfloat16),
            pltpu.VMEM((rows, rows), jnp.float32),
            pltpu.VMEM((1, rows), jnp.int32),
            pltpu.SMEM(plan.shape, jnp.int32),
            pltpu.SemaphoreType.DMA((4,)),
            pltpu.SemaphoreType.DMA((slots,)),
            pltpu.SemaphoreType.DMA((slots,)),
            pltpu.SemaphoreType.DMA((4, slots // 2)),
            pltpu.SemaphoreType.DMA((4, slots // 2)),
        ],
        compiler_params=pltpu.CompilerParams(
            collective_id=0, has_side_effects=True, vmem_limit_bytes=60 << 20
        ),
        cost_estimate=pl.CostEstimate(
            flops=8 * slots * rows * rows * width,
            bytes_accessed=4 * rows * width * 4,
            transcendentals=2 * slots * rows * rows,
        ),
    )(views_a, views_b, positives.reshape(1, rows), plan)


def solution(mesh):
    placed = (P(("grp", "dev"), None), P(("grp", "dev"), None), P(("grp", "dev")), P())
    return jax.shard_map(
        shards,
        mesh=mesh,
        in_specs=placed,
        out_specs=(P(("grp", "dev"), None), P(("grp", "dev"), None)),
        check_vma=False,
    )
```

```python
import functools
import math

import jax
import jax.numpy as jnp
from jax import lax
from jax.experimental import pallas as pl
from jax.experimental.pallas import tpu as pltpu
from jax.sharding import PartitionSpec as P

logit_scale = 2.0
logit_bias = -6.0

MESH = pl.DeviceIdType.MESH
RIGHT, LEFT, CROSS, SIBLING = range(4)
EXTRA = 16


def dot_rows(left, right):
    return lax.dot_general(left, right, (((1,), (1,)), ((), ())), preferred_element_type=jnp.float32)


def kernel(
    n, factor, a_in, b_in, labels_in, plan_in, out_a, out_b,
    held_a, held_b, scaled_a, scaled_b, offsets, labels_held, plan,
    own_sems, recv_a, recv_b, send_a, send_b,
):
    rows, width = a_in.shape
    half = n // 2
    group, member = lax.axis_index("grp"), lax.axis_index("dev")
    x, core = lax.div(group, 2), lax.rem(group, 2)
    groups = (group, (1 - x) * 2 + core, x * 2 + 1 - core, (1 - x) * 2 + 1 - core)

    odd, pair = lax.rem(member, 2), lax.div(member, 2)
    place = (1 - odd) * pair + odd * (n - 1 - pair)

    def member_at(spot):
        back = lax.div(spot, half)
        return (1 - back) * 2 * spot + back * (2 * (n - 1 - spot) + 1)

    targets = (
        (group, member_at(lax.rem(place + 1, n))),
        (group, member_at(lax.rem(place + n - 1, n))),
        (groups[1], member),
        (groups[2], member),
    )

    def behind(step):
        return lax.rem(place + n - step, n)

    def ahead(step):
        return lax.rem(place + step, n)

    def copy(side, q, spot, kind):
        held, recv, send = ((held_a, recv_a, send_a), (held_b, recv_b, send_b))[side]
        slot = spot * 4 + groups[q]
        return pltpu.make_async_remote_copy(
            src_ref=held.at[slot],
            dst_ref=held.at[slot],
            send_sem=send.at[kind, (q % 2) * n + spot],
            recv_sem=recv.at[slot],
            device_id=targets[kind],
            device_id_type=MESH,
        )

    def arrived(side, q, spot):
        copy(side, q, spot, SIBLING).wait_recv()

    def start(side, q, spot, kind):
        copy(side, q, spot, kind).start()

    def sent(side, q, spot, kind):
        copy(side, q, spot, kind).wait_send()

    def send_b_behind(step, act, first=None):
        @pl.when(step < half)
        def _():
            spot = behind(step)
            if first is not None:
                first(1, 0, spot)

            @pl.when(step < half - 1)
            def _():
                act(1, 0, spot, RIGHT)

            act(1, 0, spot, CROSS)
            act(1, 0, spot, SIBLING)

    def send_b_ahead(step, act, first=None):
        @pl.when(step <= half)
        def _():
            spot = ahead(step)
            if first is not None:
                first(1, 0, spot)

            @pl.when(step < half)
            def _():
                act(1, 0, spot, LEFT)

            act(1, 0, spot, CROSS)
            act(1, 0, spot, SIBLING)

    def send_a_behind(q, step, act, first=None):
        farthest = half - q

        @pl.when(step <= farthest)
        def _():
            spot = behind(step)
            if first is not None:
                first(0, q, spot)

            @pl.when(step < farthest)
            def _():
                act(0, q, spot, RIGHT)

            if q == 0:

                @pl.when(step == half)
                def _():
                    act(0, q, spot, CROSS)

            act(0, q, spot, SIBLING)

    def send_a_ahead(q, step, act, first=None):
        @pl.when(step < half)
        def _():
            spot = ahead(step)
            if first is not None:
                first(0, q, spot)

            @pl.when(step < half - 1)
            def _():
                act(0, q, spot, LEFT)

            act(0, q, spot, SIBLING)

    def send_own(act):
        act(0, 0, place, CROSS)
        act(0, 0, place, RIGHT)
        act(1, 0, place, LEFT)
        if half > 1:
            act(1, 0, place, RIGHT)
            act(0, 0, place, LEFT)
        act(1, 0, place, CROSS)
        act(0, 0, place, SIBLING)
        act(1, 0, place, SIBLING)

    def send_crossed(act):
        if half > 1:
            act(0, 1, place, RIGHT)
            act(0, 1, place, LEFT)
        act(0, 1, place, SIBLING)

    barrier = pltpu.get_barrier_semaphore()
    for target in targets:
        pl.semaphore_signal(barrier, inc=1, device_id=target, device_id_type=MESH)

    mine = place * 4 + group
    loads = (
        pltpu.make_async_copy(a_in, held_a.at[mine, 0:rows, :], own_sems.at[0]),
        pltpu.make_async_copy(b_in, held_b.at[mine], own_sems.at[1]),
        pltpu.make_async_copy(labels_in, labels_held, own_sems.at[2]),
        pltpu.make_async_copy(plan_in, plan, own_sems.at[3]),
    )
    for load in loads:
        load.start()
    for load in loads:
        load.wait()
    labels = labels_held[...]
    high = lax.shift_right_logical(labels, 8).astype(jnp.float32)
    low = jnp.bitwise_and(labels, 255).astype(jnp.float32)
    line = lax.broadcasted_iota(jnp.int32, (EXTRA, rows), 0)
    coded = jnp.where(line == 0, high, jnp.where(line == 1, low, 0.0))
    held_a[mine, rows : rows + EXTRA, :] = coded.astype(jnp.bfloat16)
    pl.semaphore_wait(barrier, 4)
    send_own(start)

    own_a, own_b = held_a[mine, 0:rows, :], held_b[mine]
    scaled_a[...] = (own_a.astype(jnp.float32) * (0.5 * factor)).astype(jnp.bfloat16)
    scaled_b[...] = (own_b.astype(jnp.float32) * (0.5 * factor)).astype(jnp.bfloat16)
    column = lax.broadcasted_iota(jnp.int32, (rows, rows), 1).astype(jnp.float32)
    offsets[...] = (
        jnp.transpose(jnp.broadcast_to(labels.astype(jnp.float32), (rows, rows))) - column
    )
    out_a[...] = jnp.zeros_like(out_a)
    out_b[...] = jnp.zeros_like(out_b)
    own_first = ((group * n + member) * rows).astype(jnp.float32)

    arrived(0, 1, place)
    send_crossed(start)

    def bias_of(other):
        inside = other == group
        for slot in range(plan.shape[0]):
            inside = jnp.logical_or(inside, other == plan[slot, group])
        return jnp.where(inside, 0.5 * logit_bias, -1e30).astype(jnp.float32)

    biases = [bias_of(other) for other in range(4)]

    def work(spot):
        base = spot * 4
        at = member_at(spot) * rows
        row = lax.broadcasted_iota(jnp.int32, (rows, rows), 0).astype(jnp.float32)
        keys, queries, key_weights, query_weights = [], [], [], []
        for other in range(4):
            first = (other * n * rows + at).astype(jnp.float32)
            keys.append(held_b[base + other])
            queries.append(held_a[base + other, 0:rows, :])
            code = held_a[base + other, rows : rows + EXTRA, :].astype(jnp.float32)
            found = code[0:1] * 256.0 + code[1:2] - own_first
            twice = jnp.tanh(dot_rows(scaled_a[...], keys[-1]) + biases[other])
            twice += jnp.where(offsets[...] == first, -1.0, 1.0)
            key_weights.append(twice.astype(jnp.bfloat16))
            twice = jnp.tanh(dot_rows(scaled_b[...], queries[-1]) + biases[other])
            twice += jnp.where(found == row, -1.0, 1.0)
            query_weights.append(twice.astype(jnp.bfloat16))
        out_a[...] += jnp.dot(
            jnp.concatenate(key_weights, 1),
            jnp.concatenate(keys, 0),
            preferred_element_type=jnp.float32,
        )
        out_b[...] += jnp.dot(
            jnp.concatenate(query_weights, 1),
            jnp.concatenate(queries, 0),
            preferred_element_type=jnp.float32,
        )

    def step_body(step, carry):
        last = step - 1
        count = jnp.where(jnp.logical_or(last == 0, last == half), 1, 2)

        def spot_of(index):
            return lax.rem(place + n + (2 * index - 1) * last, n)

        def receive(q, spot):
            if q == 1:

                @pl.when(last == half)
                def _():
                    arrived(0, 1, spot)
                    start(0, 1, spot, SIBLING)

            else:
                arrived(0, q, spot)
            arrived(1, q, spot)
            if q == 1:
                start(1, 1, spot, SIBLING)

        def turn(index, carry):
            spot = spot_of(index)
            for q in (1, 2, 3):
                receive(q, spot)
            work(spot)

            @pl.when(index == 0)
            def _():
                for q in range(2):
                    send_a_behind(q, step, start, arrived)
                    send_a_ahead(q, step, start, arrived)

            return carry

        send_b_behind(step, start, arrived)
        send_b_ahead(step, start, arrived)
        lax.fori_loop(0, count, turn, 0)
        return carry

    lax.fori_loop(1, half + 2, step_body, 0)

    out_a[...] = out_a[...] * (0.5 * factor)
    out_b[...] = out_b[...] * (0.5 * factor)

    send_own(sent)
    send_crossed(sent)

    def drain_body(step, carry):
        send_b_behind(step, sent)
        send_b_ahead(step, sent)
        for q in range(2):
            send_a_behind(q, step, sent)
            send_a_ahead(q, step, sent)
        return carry

    lax.fori_loop(1, half + 1, drain_body, 0)

    def drain_crossed(spot, carry):
        sent(1, 1, spot, SIBLING)
        return carry

    lax.fori_loop(0, n, drain_crossed, 0)
    sent(0, 1, ahead(half), SIBLING)


def shards(views_a, views_b, positives, plan):
    rows, width = views_a.shape
    n = lax.axis_size("dev")
    slots = lax.axis_size("grp") * n
    factor = logit_scale / math.sqrt(width)
    held = slots * (2 * rows + EXTRA) * width * 2
    vmem = pl.BlockSpec(memory_space=pltpu.VMEM)
    out = jax.ShapeDtypeStruct((rows, width), jnp.float32)
    return pl.pallas_call(
        functools.partial(kernel, n, factor),
        out_shape=(out, out),
        in_specs=[pl.BlockSpec(memory_space=pltpu.HBM)] * 4,
        out_specs=(vmem, vmem),
        scratch_shapes=[
            pltpu.VMEM((slots, rows + EXTRA, width), jnp.bfloat16),
            pltpu.VMEM((slots, rows, width), jnp.bfloat16),
            pltpu.VMEM((rows, width), jnp.bfloat16),
            pltpu.VMEM((rows, width), jnp.bfloat16),
            pltpu.VMEM((rows, rows), jnp.float32),
            pltpu.VMEM((1, rows), jnp.int32),
            pltpu.SMEM(plan.shape, jnp.int32),
            pltpu.SemaphoreType.DMA((4,)),
            pltpu.SemaphoreType.DMA((slots,)),
            pltpu.SemaphoreType.DMA((slots,)),
            pltpu.SemaphoreType.DMA((4, slots // 2)),
            pltpu.SemaphoreType.DMA((4, slots // 2)),
        ],
        compiler_params=pltpu.CompilerParams(
            collective_id=0, has_side_effects=True, vmem_limit_bytes=60 << 20
        ),
        cost_estimate=pl.CostEstimate(
            flops=8 * slots * rows * rows * width,
            bytes_accessed=4 * rows * width * 4,
            transcendentals=2 * slots * rows * rows,
        ),
    )(views_a, views_b, positives.reshape(1, rows), plan)


def solution(mesh):
    placed = (P(("grp", "dev"), None), P(("grp", "dev"), None), P(("grp", "dev")), P())
    return jax.shard_map(
        shards,
        mesh=mesh,
        in_specs=placed,
        out_specs=(P(("grp", "dev"), None), P(("grp", "dev"), None)),
        check_vma=False,
    )
```

```python
import functools
import math

import jax
import jax.numpy as jnp
from jax import lax
from jax.experimental import pallas as pl
from jax.experimental.pallas import tpu as pltpu
from jax.sharding import PartitionSpec as P

logit_scale = 2.0
logit_bias = -6.0

MESH = pl.DeviceIdType.MESH
RIGHT, LEFT, CROSS, SIBLING = range(4)
EXTRA = 16


def dot_rows(left, right):
    return lax.dot_general(left, right, (((1,), (1,)), ((), ())), preferred_element_type=jnp.float32)


def kernel(
    n, factor, a_in, b_in, labels_in, plan_in, out_a, out_b,
    held_a, held_b, mate_a, mate_b, total_a, total_b, share_a, share_b,
    scaled_a, scaled_b, offsets, labels_held, plan,
    own_sems, recv_a, recv_b, send_a, send_b, mate_send, mate_recv,
):
    rows, width = a_in.shape
    half = n // 2
    group, member = lax.axis_index("grp"), lax.axis_index("dev")
    x, core = lax.div(group, 2), lax.rem(group, 2)
    across, mate = (1 - x) * 2 + core, x * 2 + 1 - core

    odd, pair = lax.rem(member, 2), lax.div(member, 2)
    place = (1 - odd) * pair + odd * (n - 1 - pair)

    def member_at(spot):
        back = lax.div(spot, half)
        return (1 - back) * 2 * spot + back * (2 * (n - 1 - spot) + 1)

    targets = (
        (group, member_at(lax.rem(place + 1, n))),
        (group, member_at(lax.rem(place + n - 1, n))),
        (across, member),
        (mate, member),
    )

    def behind(step):
        return lax.rem(place + n - step, n)

    def ahead(step):
        return lax.rem(place + step, n)

    def copy(side, q, spot, kind):
        held, recv, send = ((held_a, recv_a, send_a), (held_b, recv_b, send_b))[side]
        slot = spot * 2 + (x if q == 0 else 1 - x)
        return pltpu.make_async_remote_copy(
            src_ref=held.at[slot],
            dst_ref=held.at[slot],
            send_sem=send.at[kind, q * n + spot],
            recv_sem=recv.at[slot],
            device_id=targets[kind],
            device_id_type=MESH,
        )

    def arrived(side, q, spot):
        copy(side, q, spot, CROSS).wait_recv()

    def start(side, q, spot, kind):
        copy(side, q, spot, kind).start()

    def sent(side, q, spot, kind):
        copy(side, q, spot, kind).wait_send()

    def send_b_behind(step, act, first=None):
        @pl.when(step < half)
        def _():
            spot = behind(step)
            if first is not None:
                first(1, 0, spot)

            @pl.when(step < half - 1)
            def _():
                act(1, 0, spot, RIGHT)

            act(1, 0, spot, CROSS)

    def send_b_ahead(step, act, first=None):
        @pl.when(step <= half)
        def _():
            spot = ahead(step)
            if first is not None:
                first(1, 0, spot)

            @pl.when(step < half)
            def _():
                act(1, 0, spot, LEFT)

            act(1, 0, spot, CROSS)

    def send_a_behind(q, step, act, first=None):
        farthest = half - q

        @pl.when(step <= farthest)
        def _():
            spot = behind(step)
            if first is not None:
                first(0, q, spot)

            @pl.when(step < farthest)
            def _():
                act(0, q, spot, RIGHT)

            if q == 0:

                @pl.when(step == half)
                def _():
                    act(0, q, spot, CROSS)

    def send_a_ahead(q, step, act, first=None):
        @pl.when(step < half)
        def _():
            spot = ahead(step)
            if first is not None:
                first(0, q, spot)

            @pl.when(step < half - 1)
            def _():
                act(0, q, spot, LEFT)

    def send_own(act):
        act(0, 0, place, CROSS)
        act(0, 0, place, RIGHT)
        act(1, 0, place, LEFT)
        if half > 1:
            act(1, 0, place, RIGHT)
            act(0, 0, place, LEFT)
        act(1, 0, place, CROSS)

    def send_crossed(act):
        if half > 1:
            act(0, 1, place, RIGHT)
            act(0, 1, place, LEFT)

    def to_mate(source, target, index):
        return pltpu.make_async_remote_copy(
            src_ref=source,
            dst_ref=target,
            send_sem=mate_send.at[index],
            recv_sem=mate_recv.at[index],
            device_id=targets[SIBLING],
            device_id_type=MESH,
        )

    barrier = pltpu.get_barrier_semaphore()
    for target in targets:
        pl.semaphore_signal(barrier, inc=1, device_id=target, device_id_type=MESH)

    mine = place * 2 + x
    loads = (
        pltpu.make_async_copy(a_in, held_a.at[mine, 0:rows, :], own_sems.at[0]),
        pltpu.make_async_copy(b_in, held_b.at[mine], own_sems.at[1]),
        pltpu.make_async_copy(labels_in, labels_held, own_sems.at[2]),
        pltpu.make_async_copy(plan_in, plan, own_sems.at[3]),
    )
    for load in loads:
        load.start()
    for load in loads:
        load.wait()
    labels = labels_held[...]
    high = lax.shift_right_logical(labels, 8).astype(jnp.float32)
    low = jnp.bitwise_and(labels, 255).astype(jnp.float32)
    line = lax.broadcasted_iota(jnp.int32, (EXTRA, rows), 0)
    coded = jnp.where(line == 0, high, jnp.where(line == 1, low, 0.0))
    held_a[mine, rows : rows + EXTRA, :] = coded.astype(jnp.bfloat16)
    pl.semaphore_wait(barrier, 4)
    send_own(start)
    own_to_mate = (
        to_mate(held_a.at[mine], mate_a, 0),
        to_mate(held_b.at[mine], mate_b, 1),
    )
    for each in own_to_mate:
        each.start()

    def decode(code):
        code = code.astype(jnp.float32)
        return code[0:1] * 256.0 + code[1:2]

    column = lax.broadcasted_iota(jnp.int32, (rows, rows), 1).astype(jnp.float32)

    def take(index, block_a, block_b, marks):
        part = slice(index * rows, (index + 1) * rows)
        scaled_a[part] = (block_a.astype(jnp.float32) * (0.5 * factor)).astype(jnp.bfloat16)
        scaled_b[part] = (block_b.astype(jnp.float32) * (0.5 * factor)).astype(jnp.bfloat16)
        offsets[part] = jnp.transpose(jnp.broadcast_to(marks, (rows, rows))) - column

    take(0, held_a[mine, 0:rows, :], held_b[mine], labels.astype(jnp.float32))
    total_a[...] = jnp.zeros_like(total_a)
    total_b[...] = jnp.zeros_like(total_b)

    arrived(0, 1, place)
    send_crossed(start)
    for each in own_to_mate:
        each.wait_recv()
    take(1, mate_a[0:rows, :], mate_b[...], decode(mate_a[rows : rows + EXTRA, :]))

    def bias_of(one, other):
        inside = other == one
        for slot in range(plan.shape[0]):
            inside = jnp.logical_or(inside, other == plan[slot, one])
        return jnp.where(inside, 0.5 * logit_bias, -1e30).astype(jnp.float32)

    owners = (group, mate)
    others = (core, 2 + core)
    biases = [[bias_of(one, other) for one in owners] for other in others]
    firsts = [((one * n + member) * rows).astype(jnp.float32) for one in owners]

    def work(spot):
        base = spot * 2
        at = member_at(spot) * rows
        row = lax.broadcasted_iota(jnp.int32, (rows, rows), 0).astype(jnp.float32)
        keys = [held_b[base + index] for index in range(2)]
        queries = [held_a[base + index, 0:rows, :] for index in range(2)]
        marks = [decode(held_a[base + index, rows : rows + EXTRA, :]) for index in range(2)]
        all_keys, all_queries = jnp.concatenate(keys, 0), jnp.concatenate(queries, 0)
        for index in range(2):
            part = slice(index * rows, (index + 1) * rows)
            key_weights, query_weights = [], []
            for other in range(2):
                bias = biases[other][index]
                first = (others[other] * n * rows + at).astype(jnp.float32)
                twice = jnp.tanh(dot_rows(scaled_a[part], keys[other]) + bias)
                twice += jnp.where(offsets[part] == first, -1.0, 1.0)
                key_weights.append(twice.astype(jnp.bfloat16))
                twice = jnp.tanh(dot_rows(scaled_b[part], queries[other]) + bias)
                twice += jnp.where(marks[other] - firsts[index] == row, -1.0, 1.0)
                query_weights.append(twice.astype(jnp.bfloat16))
            total_a[part] += jnp.dot(
                jnp.concatenate(key_weights, 1), all_keys, preferred_element_type=jnp.float32
            )
            total_b[part] += jnp.dot(
                jnp.concatenate(query_weights, 1), all_queries, preferred_element_type=jnp.float32
            )

    def step_body(step, carry):
        last = step - 1
        count = jnp.where(jnp.logical_or(last == 0, last == half), 1, 2)

        def turn(index, carry):
            spot = lax.rem(place + n + (2 * index - 1) * last, n)

            @pl.when(last == half)
            def _():
                arrived(0, 1, spot)

            arrived(1, 1, spot)
            work(spot)

            @pl.when(index == 0)
            def _():
                for q in range(2):
                    send_a_behind(q, step, start, arrived)
                    send_a_ahead(q, step, start, arrived)

            return carry

        send_b_behind(step, start, arrived)
        send_b_ahead(step, start, arrived)
        lax.fori_loop(0, count, turn, 0)
        return carry

    lax.fori_loop(1, half + 2, step_body, 0)

    shares = (
        to_mate(total_a.at[rows : 2 * rows], share_a, 2),
        to_mate(total_b.at[rows : 2 * rows], share_b, 3),
    )
    for each in shares:
        each.start()

    send_own(sent)
    send_crossed(sent)
    for each in own_to_mate:
        each.wait_send()

    def drain_body(step, carry):
        send_b_behind(step, sent)
        send_b_ahead(step, sent)
        for q in range(2):
            send_a_behind(q, step, sent)
            send_a_ahead(q, step, sent)
        return carry

    lax.fori_loop(1, half + 1, drain_body, 0)

    shares[0].wait_recv()
    out_a[...] = (total_a[0:rows] + share_a[...]) * (0.5 * factor)
    shares[1].wait_recv()
    out_b[...] = (total_b[0:rows] + share_b[...]) * (0.5 * factor)
    for each in shares:
        each.wait_send()


def shards(views_a, views_b, positives, plan):
    rows, width = views_a.shape
    n = lax.axis_size("dev")
    slots = 2 * n
    factor = logit_scale / math.sqrt(width)
    vmem = pl.BlockSpec(memory_space=pltpu.VMEM)
    out = jax.ShapeDtypeStruct((rows, width), jnp.float32)
    return pl.pallas_call(
        functools.partial(kernel, n, factor),
        out_shape=(out, out),
        in_specs=[pl.BlockSpec(memory_space=pltpu.HBM)] * 4,
        out_specs=(vmem, vmem),
        scratch_shapes=[
            pltpu.VMEM((slots, rows + EXTRA, width), jnp.bfloat16),
            pltpu.VMEM((slots, rows, width), jnp.bfloat16),
            pltpu.VMEM((rows + EXTRA, width), jnp.bfloat16),
            pltpu.VMEM((rows, width), jnp.bfloat16),
            pltpu.VMEM((2 * rows, width), jnp.float32),
            pltpu.VMEM((2 * rows, width), jnp.float32),
            pltpu.VMEM((rows, width), jnp.float32),
            pltpu.VMEM((rows, width), jnp.float32),
            pltpu.VMEM((2 * rows, width), jnp.bfloat16),
            pltpu.VMEM((2 * rows, width), jnp.bfloat16),
            pltpu.VMEM((2 * rows, rows), jnp.float32),
            pltpu.VMEM((1, rows), jnp.int32),
            pltpu.SMEM(plan.shape, jnp.int32),
            pltpu.SemaphoreType.DMA((4,)),
            pltpu.SemaphoreType.DMA((slots,)),
            pltpu.SemaphoreType.DMA((slots,)),
            pltpu.SemaphoreType.DMA((3, slots)),
            pltpu.SemaphoreType.DMA((3, slots)),
            pltpu.SemaphoreType.DMA((4,)),
            pltpu.SemaphoreType.DMA((4,)),
        ],
        compiler_params=pltpu.CompilerParams(
            collective_id=0, has_side_effects=True, vmem_limit_bytes=60 << 20
        ),
        cost_estimate=pl.CostEstimate(
            flops=16 * slots * rows * rows * width,
            bytes_accessed=4 * rows * width * 4,
            transcendentals=4 * slots * rows * rows,
        ),
    )(views_a, views_b, positives.reshape(1, rows), plan)


def solution(mesh):
    placed = (P(("grp", "dev"), None), P(("grp", "dev"), None), P(("grp", "dev")), P())
    return jax.shard_map(
        shards,
        mesh=mesh,
        in_specs=placed,
        out_specs=(P(("grp", "dev"), None), P(("grp", "dev"), None)),
        check_vma=False,
    )
```

```python
import functools
import math

import jax
import jax.numpy as jnp
from jax import lax
from jax.experimental import pallas as pl
from jax.experimental.pallas import tpu as pltpu
from jax.sharding import PartitionSpec as P

logit_scale = 2.0
logit_bias = -6.0

MESH = pl.DeviceIdType.MESH
RIGHT, LEFT, CROSS, SIBLING = range(4)
EXTRA = 16


def dot_rows(left, right):
    return lax.dot_general(left, right, (((1,), (1,)), ((), ())), preferred_element_type=jnp.float32)


def kernel(
    n, factor, a_in, b_in, labels_in, plan_in, out_a, out_b,
    held_a, held_b, mate_a, mate_b, total_a, total_b, share_a, share_b,
    scaled_a, scaled_b, offsets, labels_held, plan,
    own_sems, recv_a, recv_b, send_a, send_b, mate_send, mate_recv,
):
    rows, width = a_in.shape
    half = n // 2
    group, member = lax.axis_index("grp"), lax.axis_index("dev")
    x, core = lax.div(group, 2), lax.rem(group, 2)
    across, mate = (1 - x) * 2 + core, x * 2 + 1 - core

    odd, pair = lax.rem(member, 2), lax.div(member, 2)
    place = (1 - odd) * pair + odd * (n - 1 - pair)

    def member_at(spot):
        back = lax.div(spot, half)
        return (1 - back) * 2 * spot + back * (2 * (n - 1 - spot) + 1)

    targets = (
        (group, member_at(lax.rem(place + 1, n))),
        (group, member_at(lax.rem(place + n - 1, n))),
        (across, member),
        (mate, member),
    )

    def behind(step):
        return lax.rem(place + n - step, n)

    def ahead(step):
        return lax.rem(place + step, n)

    def copy(side, q, spot, kind):
        held, recv, send = ((held_a, recv_a, send_a), (held_b, recv_b, send_b))[side]
        slot = spot * 2 + (x if q == 0 else 1 - x)
        return pltpu.make_async_remote_copy(
            src_ref=held.at[slot],
            dst_ref=held.at[slot],
            send_sem=send.at[kind, q * n + spot],
            recv_sem=recv.at[slot],
            device_id=targets[kind],
            device_id_type=MESH,
        )

    def arrived(side, q, spot):
        copy(side, q, spot, CROSS).wait_recv()

    def start(side, q, spot, kind):
        copy(side, q, spot, kind).start()

    def sent(side, q, spot, kind):
        copy(side, q, spot, kind).wait_send()

    def send_b_behind(step, act, first=None):
        @pl.when(step < half)
        def _():
            spot = behind(step)
            if first is not None:
                first(1, 0, spot)

            @pl.when(step < half - 1)
            def _():
                act(1, 0, spot, RIGHT)

            act(1, 0, spot, CROSS)

    def send_b_ahead(step, act, first=None):
        @pl.when(step <= half)
        def _():
            spot = ahead(step)
            if first is not None:
                first(1, 0, spot)

            @pl.when(step < half)
            def _():
                act(1, 0, spot, LEFT)

            act(1, 0, spot, CROSS)

    def send_a_behind(q, step, act, first=None):
        farthest = half - q

        @pl.when(step <= farthest)
        def _():
            spot = behind(step)
            if first is not None:
                first(0, q, spot)

            @pl.when(step < farthest)
            def _():
                act(0, q, spot, RIGHT)

    def send_a_ahead(q, step, act, first=None):
        farthest = half - 1 + q

        @pl.when(step <= farthest)
        def _():
            spot = ahead(step)
            if first is not None:
                first(0, q, spot)

            @pl.when(step < farthest)
            def _():
                act(0, q, spot, LEFT)

    def send_own(act):
        act(1, 0, place, LEFT)
        if half > 1:
            act(1, 0, place, RIGHT)
        act(0, 0, place, CROSS)
        act(0, 0, place, RIGHT)
        if half > 1:
            act(0, 0, place, LEFT)
        act(1, 0, place, CROSS)

    def send_crossed(act):
        act(0, 1, place, LEFT)
        if half > 1:
            act(0, 1, place, RIGHT)

    def to_mate(source, target, index):
        return pltpu.make_async_remote_copy(
            src_ref=source,
            dst_ref=target,
            send_sem=mate_send.at[index],
            recv_sem=mate_recv.at[index],
            device_id=targets[SIBLING],
            device_id_type=MESH,
        )

    barrier = pltpu.get_barrier_semaphore()
    for target in targets:
        pl.semaphore_signal(barrier, inc=1, device_id=target, device_id_type=MESH)

    mine = place * 2 + x
    loads = (
        pltpu.make_async_copy(a_in, held_a.at[mine, 0:rows, :], own_sems.at[0]),
        pltpu.make_async_copy(b_in, held_b.at[mine], own_sems.at[1]),
        pltpu.make_async_copy(labels_in, labels_held, own_sems.at[2]),
        pltpu.make_async_copy(plan_in, plan, own_sems.at[3]),
    )
    for load in loads:
        load.start()
    for load in loads:
        load.wait()
    labels = labels_held[...]
    high = lax.shift_right_logical(labels, 8).astype(jnp.float32)
    low = jnp.bitwise_and(labels, 255).astype(jnp.float32)
    line = lax.broadcasted_iota(jnp.int32, (EXTRA, rows), 0)
    coded = jnp.where(line == 0, high, jnp.where(line == 1, low, 0.0))
    held_a[mine, rows : rows + EXTRA, :] = coded.astype(jnp.bfloat16)
    pl.semaphore_wait(barrier, 4)
    send_own(start)
    own_to_mate = (
        to_mate(held_a.at[mine], mate_a, 0),
        to_mate(held_b.at[mine], mate_b, 1),
    )
    for each in own_to_mate:
        each.start()

    def decode(code):
        code = code.astype(jnp.float32)
        return code[0:1] * 256.0 + code[1:2]

    column = lax.broadcasted_iota(jnp.int32, (rows, rows), 1).astype(jnp.float32)

    def take(index, block_a, block_b, marks):
        part = slice(index * rows, (index + 1) * rows)
        scaled_a[part] = (block_a.astype(jnp.float32) * (0.5 * factor)).astype(jnp.bfloat16)
        scaled_b[part] = (block_b.astype(jnp.float32) * (0.5 * factor)).astype(jnp.bfloat16)
        offsets[part] = jnp.transpose(jnp.broadcast_to(marks, (rows, rows))) - column

    take(0, held_a[mine, 0:rows, :], held_b[mine], labels.astype(jnp.float32))
    total_a[...] = jnp.zeros_like(total_a)
    total_b[...] = jnp.zeros_like(total_b)

    arrived(0, 1, place)
    send_crossed(start)
    for each in own_to_mate:
        each.wait_recv()
    take(1, mate_a[0:rows, :], mate_b[...], decode(mate_a[rows : rows + EXTRA, :]))

    def bias_of(one, other):
        inside = other == one
        for slot in range(plan.shape[0]):
            inside = jnp.logical_or(inside, other == plan[slot, one])
        return jnp.where(inside, 0.5 * logit_bias, -1e30).astype(jnp.float32)

    owners = (group, mate)
    others = (core, 2 + core)
    biases = [[bias_of(one, other) for one in owners] for other in others]
    firsts = [((one * n + member) * rows).astype(jnp.float32) for one in owners]

    def work(spot):
        base = spot * 2
        at = member_at(spot) * rows
        row = lax.broadcasted_iota(jnp.int32, (rows, rows), 0).astype(jnp.float32)
        keys = [held_b[base + index] for index in range(2)]
        queries = [held_a[base + index, 0:rows, :] for index in range(2)]
        marks = [decode(held_a[base + index, rows : rows + EXTRA, :]) for index in range(2)]
        all_keys, all_queries = jnp.concatenate(keys, 0), jnp.concatenate(queries, 0)
        for index in range(2):
            part = slice(index * rows, (index + 1) * rows)
            key_weights, query_weights = [], []
            for other in range(2):
                bias = biases[other][index]
                first = (others[other] * n * rows + at).astype(jnp.float32)
                twice = jnp.tanh(dot_rows(scaled_a[part], keys[other]) + bias)
                twice += jnp.where(offsets[part] == first, -1.0, 1.0)
                key_weights.append(twice.astype(jnp.bfloat16))
                twice = jnp.tanh(dot_rows(scaled_b[part], queries[other]) + bias)
                twice += jnp.where(marks[other] - firsts[index] == row, -1.0, 1.0)
                query_weights.append(twice.astype(jnp.bfloat16))
            total_a[part] += jnp.dot(
                jnp.concatenate(key_weights, 1), all_keys, preferred_element_type=jnp.float32
            )
            total_b[part] += jnp.dot(
                jnp.concatenate(query_weights, 1), all_queries, preferred_element_type=jnp.float32
            )

    def step_body(step, carry):
        last = step - 1
        count = jnp.where(jnp.logical_or(last == 0, last == half), 1, 2)

        def turn(index, carry):
            spot = lax.rem(place + n + (2 * index - 1) * last, n)
            arrived(1, 1, spot)
            work(spot)

            @pl.when(index == 0)
            def _():
                send_a_behind(0, step, start, arrived)
                send_a_ahead(0, step, start, arrived)
                send_b_behind(2 * step, start, arrived)
                send_b_ahead(2 * step, start, arrived)

            return carry

        send_b_behind(2 * step - 1, start, arrived)
        send_b_ahead(2 * step - 1, start, arrived)
        lax.fori_loop(0, count, turn, 0)
        send_a_behind(1, step, start, arrived)
        send_a_ahead(1, step, start, arrived)
        return carry

    lax.fori_loop(1, half + 2, step_body, 0)

    shares = (
        to_mate(total_a.at[rows : 2 * rows], share_a, 2),
        to_mate(total_b.at[rows : 2 * rows], share_b, 3),
    )
    for each in shares:
        each.start()

    send_own(sent)
    send_crossed(sent)
    for each in own_to_mate:
        each.wait_send()

    def drain_body(step, carry):
        send_b_behind(step, sent)
        send_b_ahead(step, sent)
        for q in range(2):
            send_a_behind(q, step, sent)
            send_a_ahead(q, step, sent)
        return carry

    lax.fori_loop(1, half + 1, drain_body, 0)

    shares[0].wait_recv()
    out_a[...] = (total_a[0:rows] + share_a[...]) * (0.5 * factor)
    shares[1].wait_recv()
    out_b[...] = (total_b[0:rows] + share_b[...]) * (0.5 * factor)
    for each in shares:
        each.wait_send()


def shards(views_a, views_b, positives, plan):
    rows, width = views_a.shape
    n = lax.axis_size("dev")
    slots = 2 * n
    factor = logit_scale / math.sqrt(width)
    vmem = pl.BlockSpec(memory_space=pltpu.VMEM)
    out = jax.ShapeDtypeStruct((rows, width), jnp.float32)
    return pl.pallas_call(
        functools.partial(kernel, n, factor),
        out_shape=(out, out),
        in_specs=[pl.BlockSpec(memory_space=pltpu.HBM)] * 4,
        out_specs=(vmem, vmem),
        scratch_shapes=[
            pltpu.VMEM((slots, rows + EXTRA, width), jnp.bfloat16),
            pltpu.VMEM((slots, rows, width), jnp.bfloat16),
            pltpu.VMEM((rows + EXTRA, width), jnp.bfloat16),
            pltpu.VMEM((rows, width), jnp.bfloat16),
            pltpu.VMEM((2 * rows, width), jnp.float32),
            pltpu.VMEM((2 * rows, width), jnp.float32),
            pltpu.VMEM((rows, width), jnp.float32),
            pltpu.VMEM((rows, width), jnp.float32),
            pltpu.VMEM((2 * rows, width), jnp.bfloat16),
            pltpu.VMEM((2 * rows, width), jnp.bfloat16),
            pltpu.VMEM((2 * rows, rows), jnp.float32),
            pltpu.VMEM((1, rows), jnp.int32),
            pltpu.SMEM(plan.shape, jnp.int32),
            pltpu.SemaphoreType.DMA((4,)),
            pltpu.SemaphoreType.DMA((slots,)),
            pltpu.SemaphoreType.DMA((slots,)),
            pltpu.SemaphoreType.DMA((3, slots)),
            pltpu.SemaphoreType.DMA((3, slots)),
            pltpu.SemaphoreType.DMA((4,)),
            pltpu.SemaphoreType.DMA((4,)),
        ],
        compiler_params=pltpu.CompilerParams(
            collective_id=0, has_side_effects=True, vmem_limit_bytes=60 << 20
        ),
        cost_estimate=pl.CostEstimate(
            flops=16 * slots * rows * rows * width,
            bytes_accessed=4 * rows * width * 4,
            transcendentals=4 * slots * rows * rows,
        ),
    )(views_a, views_b, positives.reshape(1, rows), plan)


def solution(mesh):
    placed = (P(("grp", "dev"), None), P(("grp", "dev"), None), P(("grp", "dev")), P())
    return jax.shard_map(
        shards,
        mesh=mesh,
        in_specs=placed,
        out_specs=(P(("grp", "dev"), None), P(("grp", "dev"), None)),
        check_vma=False,
    )
```

```python
import functools
import math

import jax
import jax.numpy as jnp
from jax import lax
from jax.experimental import pallas as pl
from jax.experimental.pallas import tpu as pltpu
from jax.sharding import PartitionSpec as P

logit_scale = 2.0
logit_bias = -6.0

MESH = pl.DeviceIdType.MESH
RIGHT, LEFT, CROSS, SIBLING = range(4)
EXTRA = 16


def dot_rows(left, right):
    return lax.dot_general(left, right, (((1,), (1,)), ((), ())), preferred_element_type=jnp.float32)


def kernel(
    n, factor, a_in, b_in, labels_in, plan_in, out_a, out_b,
    held_a, held_b, mate_a, mate_b, total_a, total_b, share_a, share_b,
    scaled_a, scaled_b, offsets, labels_held, plan,
    own_sems, recv_a, recv_b, send_a, send_b, mate_send, mate_recv,
):
    rows, width = a_in.shape
    half = n // 2
    group, member = lax.axis_index("grp"), lax.axis_index("dev")
    x, core = lax.div(group, 2), lax.rem(group, 2)
    across, mate = (1 - x) * 2 + core, x * 2 + 1 - core

    odd, pair = lax.rem(member, 2), lax.div(member, 2)
    place = (1 - odd) * pair + odd * (n - 1 - pair)

    def member_at(spot):
        back = lax.div(spot, half)
        return (1 - back) * 2 * spot + back * (2 * (n - 1 - spot) + 1)

    targets = (
        (group, member_at(lax.rem(place + 1, n))),
        (group, member_at(lax.rem(place + n - 1, n))),
        (across, member),
        (mate, member),
    )

    def behind(step):
        return lax.rem(place + n - step, n)

    def ahead(step):
        return lax.rem(place + step, n)

    def copy(side, q, spot, kind):
        held, recv, send = ((held_a, recv_a, send_a), (held_b, recv_b, send_b))[side]
        slot = spot * 2 + (x if q == 0 else 1 - x)
        return pltpu.make_async_remote_copy(
            src_ref=held.at[slot],
            dst_ref=held.at[slot],
            send_sem=send.at[kind, q * n + spot],
            recv_sem=recv.at[slot],
            device_id=targets[kind],
            device_id_type=MESH,
        )

    def arrived(side, q, spot):
        copy(side, q, spot, CROSS).wait_recv()

    def start(side, q, spot, kind):
        copy(side, q, spot, kind).start()

    def sent(side, q, spot, kind):
        copy(side, q, spot, kind).wait_send()

    def send_b_behind(step, act, first=None):
        @pl.when(step < half)
        def _():
            spot = behind(step)
            if first is not None:
                first(1, 0, spot)

            @pl.when(step < half - 1)
            def _():
                act(1, 0, spot, RIGHT)

            act(1, 0, spot, CROSS)

    def send_b_ahead(step, act, first=None):
        @pl.when(step <= half)
        def _():
            spot = ahead(step)
            if first is not None:
                first(1, 0, spot)

            @pl.when(step < half)
            def _():
                act(1, 0, spot, LEFT)

            act(1, 0, spot, CROSS)

    def send_a_behind(q, step, act, first=None):
        farthest = half - q

        @pl.when(step <= farthest)
        def _():
            spot = behind(step)
            if first is not None:
                first(0, q, spot)

            @pl.when(step < farthest)
            def _():
                act(0, q, spot, RIGHT)

    def send_a_ahead(q, step, act, first=None):
        farthest = half - 1 + q

        @pl.when(step <= farthest)
        def _():
            spot = ahead(step)
            if first is not None:
                first(0, q, spot)

            @pl.when(step < farthest)
            def _():
                act(0, q, spot, LEFT)

    def send_own(act):
        act(1, 0, place, LEFT)
        if half > 1:
            act(1, 0, place, RIGHT)
        act(0, 0, place, CROSS)
        act(0, 0, place, RIGHT)
        if half > 1:
            act(0, 0, place, LEFT)
        act(1, 0, place, CROSS)

    def send_crossed(act):
        act(0, 1, place, LEFT)
        if half > 1:
            act(0, 1, place, RIGHT)

    def to_mate(source, target, index):
        return pltpu.make_async_remote_copy(
            src_ref=source,
            dst_ref=target,
            send_sem=mate_send.at[index],
            recv_sem=mate_recv.at[index],
            device_id=targets[SIBLING],
            device_id_type=MESH,
        )

    barrier = pltpu.get_barrier_semaphore()
    for target in targets:
        pl.semaphore_signal(barrier, inc=1, device_id=target, device_id_type=MESH)

    mine = place * 2 + x
    loads = (
        pltpu.make_async_copy(a_in, held_a.at[mine, 0:rows, :], own_sems.at[0]),
        pltpu.make_async_copy(b_in, held_b.at[mine], own_sems.at[1]),
        pltpu.make_async_copy(labels_in, labels_held, own_sems.at[2]),
        pltpu.make_async_copy(plan_in, plan, own_sems.at[3]),
    )
    for load in loads:
        load.start()
    for load in loads:
        load.wait()
    labels = labels_held[...]
    high = lax.shift_right_logical(labels, 8).astype(jnp.float32)
    low = jnp.bitwise_and(labels, 255).astype(jnp.float32)
    line = lax.broadcasted_iota(jnp.int32, (EXTRA, rows), 0)
    coded = jnp.where(line == 0, high, jnp.where(line == 1, low, 0.0))
    held_a[mine, rows : rows + EXTRA, :] = coded.astype(jnp.bfloat16)
    pl.semaphore_wait(barrier, 4)
    send_own(start)
    own_to_mate = (
        to_mate(held_a.at[mine], mate_a, 0),
        to_mate(held_b.at[mine], mate_b, 1),
    )
    for each in own_to_mate:
        each.start()

    def decode(code):
        code = code.astype(jnp.float32)
        return code[0:1] * 256.0 + code[1:2]

    column = lax.broadcasted_iota(jnp.int32, (rows, rows), 1).astype(jnp.float32)

    missing = sum(range(4)) - group
    for slot in range(plan.shape[0]):
        missing -= plan[slot, group]
    swap_1 = missing == across
    swap_2 = missing == 3 - group
    swaps = (None, swap_1, swap_2)

    def pick(swap, one, other):
        return lax.select(jnp.broadcast_to(swap, one.shape), one, other)

    def scale(block):
        return (block.astype(jnp.float32) * (0.5 * factor)).astype(jnp.bfloat16)

    def spread(marks):
        return jnp.transpose(jnp.broadcast_to(marks, (rows, rows))) - column

    def part_of(index):
        return slice(index * rows, (index + 1) * rows)

    scaled_a[part_of(0)] = scale(held_a[mine, 0:rows, :])
    scaled_b[part_of(0)] = scale(held_b[mine])
    offsets[part_of(0)] = spread(labels.astype(jnp.float32))
    total_a[...] = jnp.zeros_like(total_a)
    total_b[...] = jnp.zeros_like(total_b)

    arrived(0, 1, place)
    send_crossed(start)
    for each in own_to_mate:
        each.wait_recv()
    scaled_a[part_of(2)] = scale(mate_a[0:rows, :])
    scaled_b[part_of(2)] = scale(mate_b[...])
    offsets[part_of(2)] = spread(decode(mate_a[rows : rows + EXTRA, :]))
    for ref in (scaled_a, scaled_b, offsets):
        ref[part_of(1)] = pick(swap_1, ref[part_of(2)], ref[part_of(0)])

    owners = (group, jnp.where(swap_1, mate, group), mate)
    others = (group, jnp.where(swap_1, group, across), jnp.where(swap_2, group, across))
    own_firsts = [((one * n + member) * rows).astype(jnp.float32) for one in owners]

    def work(spot):
        base = spot * 2
        at = member_at(spot) * rows
        row = lax.broadcasted_iota(jnp.int32, (rows, rows), 0).astype(jnp.float32)
        near, far = base + x, base + 1 - x
        near_keys, far_keys = held_b[near], held_b[far]
        near_queries, far_queries = held_a[near, 0:rows, :], held_a[far, 0:rows, :]
        near_marks = decode(held_a[near, rows : rows + EXTRA, :])
        far_marks = decode(held_a[far, rows : rows + EXTRA, :])
        for index in range(3):
            part = part_of(index)
            keys, queries, marks = near_keys, near_queries, near_marks
            if index > 0:
                keys = pick(swaps[index], near_keys, far_keys)
                queries = pick(swaps[index], near_queries, far_queries)
                marks = pick(swaps[index], near_marks, far_marks)
            first = (others[index] * n * rows + at).astype(jnp.float32)
            twice = jnp.tanh(dot_rows(scaled_a[part], keys) + 0.5 * logit_bias)
            twice += jnp.where(offsets[part] == first, -1.0, 1.0)
            total_a[part] += jnp.dot(
                twice.astype(jnp.bfloat16), keys, preferred_element_type=jnp.float32
            )
            twice = jnp.tanh(dot_rows(scaled_b[part], queries) + 0.5 * logit_bias)
            twice += jnp.where(marks - own_firsts[index] == row, -1.0, 1.0)
            total_b[part] += jnp.dot(
                twice.astype(jnp.bfloat16), queries, preferred_element_type=jnp.float32
            )

    def step_body(step, carry):
        last = step - 1
        count = jnp.where(jnp.logical_or(last == 0, last == half), 1, 2)

        def turn(index, carry):
            spot = lax.rem(place + n + (2 * index - 1) * last, n)
            arrived(1, 1, spot)
            work(spot)

            @pl.when(index == 0)
            def _():
                send_a_behind(0, step, start, arrived)
                send_a_ahead(0, step, start, arrived)
                send_b_behind(2 * step, start, arrived)
                send_b_ahead(2 * step, start, arrived)

            return carry

        send_b_behind(2 * step - 1, start, arrived)
        send_b_ahead(2 * step - 1, start, arrived)
        lax.fori_loop(0, count, turn, 0)
        send_a_behind(1, step, start, arrived)
        send_a_ahead(1, step, start, arrived)
        return carry

    lax.fori_loop(1, half + 2, step_body, 0)

    shares = (
        to_mate(total_a.at[2 * rows : 3 * rows], share_a, 2),
        to_mate(total_b.at[2 * rows : 3 * rows], share_b, 3),
    )
    for total, each in zip((total_a, total_b), shares):
        middle = total[part_of(1)]
        nothing = jnp.zeros_like(middle)
        total[part_of(2)] += pick(swap_1, middle, nothing)
        each.start()
        total[part_of(0)] += pick(swap_1, nothing, middle)

    send_own(sent)
    send_crossed(sent)
    for each in own_to_mate:
        each.wait_send()

    def drain_body(step, carry):
        send_b_behind(step, sent)
        send_b_ahead(step, sent)
        for q in range(2):
            send_a_behind(q, step, sent)
            send_a_ahead(q, step, sent)
        return carry

    lax.fori_loop(1, half + 1, drain_body, 0)

    shares[0].wait_recv()
    out_a[...] = (total_a[0:rows] + share_a[...]) * (0.5 * factor)
    shares[1].wait_recv()
    out_b[...] = (total_b[0:rows] + share_b[...]) * (0.5 * factor)
    for each in shares:
        each.wait_send()


def shards(views_a, views_b, positives, plan):
    rows, width = views_a.shape
    n = lax.axis_size("dev")
    slots = 2 * n
    factor = logit_scale / math.sqrt(width)
    vmem = pl.BlockSpec(memory_space=pltpu.VMEM)
    out = jax.ShapeDtypeStruct((rows, width), jnp.float32)
    return pl.pallas_call(
        functools.partial(kernel, n, factor),
        out_shape=(out, out),
        in_specs=[pl.BlockSpec(memory_space=pltpu.HBM)] * 4,
        out_specs=(vmem, vmem),
        scratch_shapes=[
            pltpu.VMEM((slots, rows + EXTRA, width), jnp.bfloat16),
            pltpu.VMEM((slots, rows, width), jnp.bfloat16),
            pltpu.VMEM((rows + EXTRA, width), jnp.bfloat16),
            pltpu.VMEM((rows, width), jnp.bfloat16),
            pltpu.VMEM((3 * rows, width), jnp.float32),
            pltpu.VMEM((3 * rows, width), jnp.float32),
            pltpu.VMEM((rows, width), jnp.float32),
            pltpu.VMEM((rows, width), jnp.float32),
            pltpu.VMEM((3 * rows, width), jnp.bfloat16),
            pltpu.VMEM((3 * rows, width), jnp.bfloat16),
            pltpu.VMEM((3 * rows, rows), jnp.float32),
            pltpu.VMEM((1, rows), jnp.int32),
            pltpu.SMEM(plan.shape, jnp.int32),
            pltpu.SemaphoreType.DMA((4,)),
            pltpu.SemaphoreType.DMA((slots,)),
            pltpu.SemaphoreType.DMA((slots,)),
            pltpu.SemaphoreType.DMA((3, slots)),
            pltpu.SemaphoreType.DMA((3, slots)),
            pltpu.SemaphoreType.DMA((4,)),
            pltpu.SemaphoreType.DMA((4,)),
        ],
        compiler_params=pltpu.CompilerParams(
            collective_id=0, has_side_effects=True, vmem_limit_bytes=60 << 20
        ),
        cost_estimate=pl.CostEstimate(
            flops=12 * slots * rows * rows * width,
            bytes_accessed=4 * rows * width * 4,
            transcendentals=3 * slots * rows * rows,
        ),
    )(views_a, views_b, positives.reshape(1, rows), plan)


def solution(mesh):
    placed = (P(("grp", "dev"), None), P(("grp", "dev"), None), P(("grp", "dev")), P())
    return jax.shard_map(
        shards,
        mesh=mesh,
        in_specs=placed,
        out_specs=(P(("grp", "dev"), None), P(("grp", "dev"), None)),
        check_vma=False,
    )
```

```python
import functools
import math

import jax
import jax.numpy as jnp
from jax import lax
from jax.experimental import pallas as pl
from jax.experimental.pallas import tpu as pltpu
from jax.sharding import PartitionSpec as P

logit_scale = 2.0
logit_bias = -6.0

MESH = pl.DeviceIdType.MESH
RIGHT, LEFT, CROSS, SIBLING = range(4)
EXTRA = 16


def dot_rows(left, right):
    return lax.dot_general(left, right, (((1,), (1,)), ((), ())), preferred_element_type=jnp.float32)


def kernel(
    n, factor, a_in, b_in, labels_in, plan_in, own_a, own_b, share_a, share_b,
    held_a, held_b, mate_a, mate_b, total_a, total_b,
    scaled_a, scaled_b, offsets, labels_held, plan,
    own_sems, recv_a, recv_b, send_a, send_b, mate_send, mate_recv,
):
    rows, width = a_in.shape
    half = n // 2
    group, member = lax.axis_index("grp"), lax.axis_index("dev")
    x, core = lax.div(group, 2), lax.rem(group, 2)
    across, mate = (1 - x) * 2 + core, x * 2 + 1 - core

    odd, pair = lax.rem(member, 2), lax.div(member, 2)
    place = (1 - odd) * pair + odd * (n - 1 - pair)

    def member_at(spot):
        back = lax.div(spot, half)
        return (1 - back) * 2 * spot + back * (2 * (n - 1 - spot) + 1)

    targets = (
        (group, member_at(lax.rem(place + 1, n))),
        (group, member_at(lax.rem(place + n - 1, n))),
        (across, member),
        (mate, member),
    )

    def behind(step):
        return lax.rem(place + n - step, n)

    def ahead(step):
        return lax.rem(place + step, n)

    def copy(side, q, spot, kind):
        held, recv, send = ((held_a, recv_a, send_a), (held_b, recv_b, send_b))[side]
        slot = spot * 2 + (x if q == 0 else 1 - x)
        return pltpu.make_async_remote_copy(
            src_ref=held.at[slot],
            dst_ref=held.at[slot],
            send_sem=send.at[kind, q * n + spot],
            recv_sem=recv.at[slot],
            device_id=targets[kind],
            device_id_type=MESH,
        )

    def arrived(side, q, spot):
        copy(side, q, spot, CROSS).wait_recv()

    def start(side, q, spot, kind):
        copy(side, q, spot, kind).start()

    def sent(side, q, spot, kind):
        copy(side, q, spot, kind).wait_send()

    def send_b_behind(step, act, first=None):
        @pl.when(step < half)
        def _():
            spot = behind(step)
            if first is not None:
                first(1, 0, spot)

            @pl.when(step < half - 1)
            def _():
                act(1, 0, spot, RIGHT)

            act(1, 0, spot, CROSS)

    def send_b_ahead(step, act, first=None):
        @pl.when(step <= half)
        def _():
            spot = ahead(step)
            if first is not None:
                first(1, 0, spot)

            @pl.when(step < half)
            def _():
                act(1, 0, spot, LEFT)

            act(1, 0, spot, CROSS)

    def send_a_behind(q, step, act, first=None):
        farthest = half - q

        @pl.when(step <= farthest)
        def _():
            spot = behind(step)
            if first is not None:
                first(0, q, spot)

            @pl.when(step < farthest)
            def _():
                act(0, q, spot, RIGHT)

            if q == 0 and half == 1:
                act(0, q, spot, CROSS)

    def send_a_ahead(q, step, act, first=None):
        farthest = half - 1 + q

        @pl.when(step <= farthest)
        def _():
            spot = ahead(step)
            if first is not None:
                first(0, q, spot)

            @pl.when(step < farthest)
            def _():
                act(0, q, spot, LEFT)

            if q == 0:

                @pl.when(step == 1)
                def _():
                    act(0, q, spot, CROSS)

    def send_own(act):
        act(1, 0, place, LEFT)
        if half > 1:
            act(1, 0, place, RIGHT)
        act(0, 0, place, CROSS)
        act(0, 0, place, RIGHT)
        if half > 1:
            act(0, 0, place, LEFT)
        act(1, 0, place, CROSS)

    def send_crossed(act):
        if half > 1:
            act(0, 1, place, RIGHT)

    def to_mate(source, target, index):
        return pltpu.make_async_remote_copy(
            src_ref=source,
            dst_ref=target,
            send_sem=mate_send.at[index],
            recv_sem=mate_recv.at[index],
            device_id=targets[SIBLING],
            device_id_type=MESH,
        )

    barrier = pltpu.get_barrier_semaphore()
    for target in targets:
        pl.semaphore_signal(barrier, inc=1, device_id=target, device_id_type=MESH)

    mine = place * 2 + x
    loads = (
        pltpu.make_async_copy(a_in, held_a.at[mine, 0:rows, :], own_sems.at[0]),
        pltpu.make_async_copy(b_in, held_b.at[mine], own_sems.at[1]),
        pltpu.make_async_copy(labels_in, labels_held, own_sems.at[2]),
        pltpu.make_async_copy(plan_in, plan, own_sems.at[3]),
    )
    for load in loads:
        load.start()
    for load in loads:
        load.wait()
    labels = labels_held[...]
    high = lax.shift_right_logical(labels, 8).astype(jnp.float32)
    low = jnp.bitwise_and(labels, 255).astype(jnp.float32)
    line = lax.broadcasted_iota(jnp.int32, (EXTRA, rows), 0)
    coded = jnp.where(line == 0, high, jnp.where(line == 1, low, 0.0))
    held_a[mine, rows : rows + EXTRA, :] = coded.astype(jnp.bfloat16)
    pl.semaphore_wait(barrier, 4)
    send_own(start)
    own_to_mate = (
        to_mate(held_a.at[mine], mate_a, 0),
        to_mate(held_b.at[mine], mate_b, 1),
    )
    for each in own_to_mate:
        each.start()

    def decode(code):
        code = code.astype(jnp.float32)
        return code[0:1] * 256.0 + code[1:2]

    column = lax.broadcasted_iota(jnp.int32, (rows, rows), 1).astype(jnp.float32)

    missing = sum(range(4)) - group
    for slot in range(plan.shape[0]):
        missing -= plan[slot, group]
    swap_1 = missing == across
    swap_2 = missing == 3 - group
    swaps = (None, swap_1, swap_2)

    def pick(swap, one, other):
        return lax.select(jnp.broadcast_to(swap, one.shape), one, other)

    def scale(block):
        return (block.astype(jnp.float32) * (0.5 * factor)).astype(jnp.bfloat16)

    def spread(marks):
        return jnp.transpose(jnp.broadcast_to(marks, (rows, rows))) - column

    def part_of(index):
        return slice(index * rows, (index + 1) * rows)

    scaled_a[part_of(0)] = scale(held_a[mine, 0:rows, :])
    scaled_b[part_of(0)] = scale(held_b[mine])
    offsets[part_of(0)] = spread(labels.astype(jnp.float32))
    total_a[...] = jnp.zeros_like(total_a)
    total_b[...] = jnp.zeros_like(total_b)

    arrived(0, 1, place)
    send_crossed(start)
    for each in own_to_mate:
        each.wait_recv()
    scaled_a[part_of(2)] = scale(mate_a[0:rows, :])
    scaled_b[part_of(2)] = scale(mate_b[...])
    offsets[part_of(2)] = spread(decode(mate_a[rows : rows + EXTRA, :]))
    for ref in (scaled_a, scaled_b, offsets):
        ref[part_of(1)] = pick(swap_1, ref[part_of(2)], ref[part_of(0)])

    owners = (group, jnp.where(swap_1, mate, group), mate)
    others = (group, jnp.where(swap_1, group, across), jnp.where(swap_2, group, across))
    own_firsts = [((one * n + member) * rows).astype(jnp.float32) for one in owners]

    def work(spot):
        base = spot * 2
        at = member_at(spot) * rows
        row = lax.broadcasted_iota(jnp.int32, (rows, rows), 0).astype(jnp.float32)
        near, far = base + x, base + 1 - x
        near_keys, far_keys = held_b[near], held_b[far]
        near_queries, far_queries = held_a[near, 0:rows, :], held_a[far, 0:rows, :]
        near_marks = decode(held_a[near, rows : rows + EXTRA, :])
        far_marks = decode(held_a[far, rows : rows + EXTRA, :])
        for index in range(3):
            part = part_of(index)
            keys, queries, marks = near_keys, near_queries, near_marks
            if index > 0:
                keys = pick(swaps[index], near_keys, far_keys)
                queries = pick(swaps[index], near_queries, far_queries)
                marks = pick(swaps[index], near_marks, far_marks)
            first = (others[index] * n * rows + at).astype(jnp.float32)
            twice = jnp.tanh(dot_rows(scaled_a[part], keys) + 0.5 * logit_bias)
            twice += jnp.where(offsets[part] == first, -1.0, 1.0)
            total_a[part] += jnp.dot(
                twice.astype(jnp.bfloat16), keys, preferred_element_type=jnp.float32
            )
            twice = jnp.tanh(dot_rows(scaled_b[part], queries) + 0.5 * logit_bias)
            twice += jnp.where(marks - own_firsts[index] == row, -1.0, 1.0)
            total_b[part] += jnp.dot(
                twice.astype(jnp.bfloat16), queries, preferred_element_type=jnp.float32
            )

    def step_body(step, carry):
        last = step - 1
        count = jnp.where(jnp.logical_or(last == 0, last == half), 1, 2)

        def turn(index, carry):
            spot = lax.rem(place + n + (2 * index - 1) * last, n)
            arrived(1, 1, spot)
            work(spot)

            @pl.when(index == 0)
            def _():
                send_a_behind(0, step, start, arrived)
                send_a_ahead(0, step, start, arrived)
                send_b_behind(2 * step, start, arrived)
                send_b_ahead(2 * step, start, arrived)

            return carry

        send_b_behind(2 * step - 1, start, arrived)
        send_b_ahead(2 * step - 1, start, arrived)
        lax.fori_loop(0, count, turn, 0)
        send_a_behind(1, step, start, arrived)
        send_a_ahead(1, step, start, arrived)
        return carry

    lax.fori_loop(1, half + 2, step_body, 0)

    shares = (
        to_mate(total_a.at[2 * rows : 3 * rows], share_a, 2),
        to_mate(total_b.at[2 * rows : 3 * rows], share_b, 3),
    )
    stores = (
        pltpu.make_async_copy(total_a.at[0:rows], own_a, own_sems.at[0]),
        pltpu.make_async_copy(total_b.at[0:rows], own_b, own_sems.at[1]),
    )
    for total, share, store in zip((total_a, total_b), shares, stores):
        middle = total[part_of(1)]
        nothing = jnp.zeros_like(middle)
        total[part_of(2)] += pick(swap_1, middle, nothing)
        share.start()
        total[part_of(0)] += pick(swap_1, nothing, middle)
        store.start()

    send_own(sent)
    send_crossed(sent)
    for each in own_to_mate:
        each.wait_send()

    def drain_body(step, carry):
        send_b_behind(step, sent)
        send_b_ahead(step, sent)
        for q in range(2):
            send_a_behind(q, step, sent)
            send_a_ahead(q, step, sent)
        return carry

    lax.fori_loop(1, half + 1, drain_body, 0)

    for store in stores:
        store.wait()
    for share in shares:
        share.wait_recv()
        share.wait_send()


def finish(factor, own_a, own_b, share_a, share_b, out_a, out_b):
    out_a[...] = (own_a[...] + share_a[...]) * (0.5 * factor)
    out_b[...] = (own_b[...] + share_b[...]) * (0.5 * factor)


def shards(views_a, views_b, positives, plan):
    rows, width = views_a.shape
    n = lax.axis_size("dev")
    slots = 2 * n
    factor = logit_scale / math.sqrt(width)
    vmem, hbm = (pl.BlockSpec(memory_space=space) for space in (pltpu.VMEM, pl.ANY))
    out = jax.ShapeDtypeStruct((rows, width), jnp.float32)
    sums = pl.pallas_call(
        functools.partial(kernel, n, factor),
        out_shape=(out,) * 4,
        in_specs=[hbm] * 4,
        out_specs=(hbm,) * 4,
        scratch_shapes=[
            pltpu.VMEM((slots, rows + EXTRA, width), jnp.bfloat16),
            pltpu.VMEM((slots, rows, width), jnp.bfloat16),
            pltpu.VMEM((rows + EXTRA, width), jnp.bfloat16),
            pltpu.VMEM((rows, width), jnp.bfloat16),
            pltpu.VMEM((3 * rows, width), jnp.float32),
            pltpu.VMEM((3 * rows, width), jnp.float32),
            pltpu.VMEM((3 * rows, width), jnp.bfloat16),
            pltpu.VMEM((3 * rows, width), jnp.bfloat16),
            pltpu.VMEM((3 * rows, rows), jnp.float32),
            pltpu.VMEM((1, rows), jnp.int32),
            pltpu.SMEM(plan.shape, jnp.int32),
            pltpu.SemaphoreType.DMA((4,)),
            pltpu.SemaphoreType.DMA((slots,)),
            pltpu.SemaphoreType.DMA((slots,)),
            pltpu.SemaphoreType.DMA((3, slots)),
            pltpu.SemaphoreType.DMA((3, slots)),
            pltpu.SemaphoreType.DMA((4,)),
            pltpu.SemaphoreType.DMA((4,)),
        ],
        compiler_params=pltpu.CompilerParams(
            collective_id=0, has_side_effects=True, vmem_limit_bytes=60 << 20
        ),
        cost_estimate=pl.CostEstimate(
            flops=12 * slots * rows * rows * width,
            bytes_accessed=4 * rows * width * 4,
            transcendentals=3 * slots * rows * rows,
        ),
    )(views_a, views_b, positives.reshape(1, rows), plan)
    return pl.pallas_call(
        functools.partial(finish, factor),
        out_shape=(out, out),
        in_specs=[vmem] * 4,
        out_specs=(vmem, vmem),
        compiler_params=pltpu.CompilerParams(vmem_limit_bytes=60 << 20),
    )(*sums)


def solution(mesh):
    placed = (P(("grp", "dev"), None), P(("grp", "dev"), None), P(("grp", "dev")), P())
    return jax.shard_map(
        shards,
        mesh=mesh,
        in_specs=placed,
        out_specs=(P(("grp", "dev"), None), P(("grp", "dev"), None)),
        check_vma=False,
    )
```

```python
import functools
import math

import jax
import jax.numpy as jnp
from jax import lax
from jax.experimental import pallas as pl
from jax.experimental.pallas import tpu as pltpu
from jax.sharding import PartitionSpec as P

logit_scale = 2.0
logit_bias = -6.0

MESH = pl.DeviceIdType.MESH
RIGHT, LEFT, CROSS, SIBLING = range(4)
EXTRA = 16


def dot_rows(left, right):
    return lax.dot_general(left, right, (((1,), (1,)), ((), ())), preferred_element_type=jnp.float32)


def kernel(
    n, factor, a_in, b_in, labels_in, plan_in, own_a, own_b, share_a, share_b,
    held_a, held_b, mate_a, mate_b, total_a, total_b,
    scaled_a, scaled_b, offsets, labels_held, plan,
    own_sems, recv_a, recv_b, send_a, send_b, mate_send, mate_recv,
):
    rows, width = a_in.shape
    half = n // 2
    group, member = lax.axis_index("grp"), lax.axis_index("dev")
    x, core = lax.div(group, 2), lax.rem(group, 2)
    across, mate = (1 - x) * 2 + core, x * 2 + 1 - core

    odd, pair = lax.rem(member, 2), lax.div(member, 2)
    place = (1 - odd) * pair + odd * (n - 1 - pair)

    def member_at(spot):
        back = lax.div(spot, half)
        return (1 - back) * 2 * spot + back * (2 * (n - 1 - spot) + 1)

    targets = (
        (group, member_at(lax.rem(place + 1, n))),
        (group, member_at(lax.rem(place + n - 1, n))),
        (across, member),
        (mate, member),
    )

    def behind(step):
        return lax.rem(place + n - step, n)

    def ahead(step):
        return lax.rem(place + step, n)

    def copy(side, q, spot, kind):
        held, recv, send = ((held_a, recv_a, send_a), (held_b, recv_b, send_b))[side]
        slot = spot * 2 + (x if q == 0 else 1 - x)
        return pltpu.make_async_remote_copy(
            src_ref=held.at[slot],
            dst_ref=held.at[slot],
            send_sem=send.at[kind, q * n + spot],
            recv_sem=recv.at[slot],
            device_id=targets[kind],
            device_id_type=MESH,
        )

    def arrived(side, q, spot):
        copy(side, q, spot, CROSS).wait_recv()

    def start(side, q, spot, kind):
        copy(side, q, spot, kind).start()

    def sent(side, q, spot, kind):
        copy(side, q, spot, kind).wait_send()

    def send_b_behind(step, act, first=None):
        @pl.when(step < half)
        def _():
            spot = behind(step)
            if first is not None:
                first(1, 0, spot)

            @pl.when(step < half - 1)
            def _():
                act(1, 0, spot, RIGHT)

            act(1, 0, spot, CROSS)

    def send_b_ahead(step, act, first=None):
        @pl.when(step <= half)
        def _():
            spot = ahead(step)
            if first is not None:
                first(1, 0, spot)

            @pl.when(step < half)
            def _():
                act(1, 0, spot, LEFT)

            act(1, 0, spot, CROSS)

    def send_a_behind(q, step, act, first=None):
        farthest = half - q

        @pl.when(step <= farthest)
        def _():
            spot = behind(step)
            if first is not None:
                first(0, q, spot)

            @pl.when(step < farthest)
            def _():
                act(0, q, spot, RIGHT)

            if q == 0 and half == 1:
                act(0, q, spot, CROSS)

    def send_a_ahead(q, step, act, first=None):
        farthest = half - 1 + q

        @pl.when(step <= farthest)
        def _():
            spot = ahead(step)
            if first is not None:
                first(0, q, spot)

            @pl.when(step < farthest)
            def _():
                act(0, q, spot, LEFT)

            if q == 0:

                @pl.when(step == 1)
                def _():
                    act(0, q, spot, CROSS)

    def send_own_first(act):
        act(1, 0, place, LEFT)
        if half > 1:
            act(1, 0, place, RIGHT)

    def send_own_then(act):
        act(0, 0, place, RIGHT)
        if half > 1:
            act(0, 0, place, LEFT)
        act(1, 0, place, CROSS)

    def send_crossed(act):
        if half > 1:
            act(0, 1, place, RIGHT)

    def to_mate(source, target, index):
        return pltpu.make_async_remote_copy(
            src_ref=source,
            dst_ref=target,
            send_sem=mate_send.at[index],
            recv_sem=mate_recv.at[index],
            device_id=targets[SIBLING],
            device_id_type=MESH,
        )

    barrier = pltpu.get_barrier_semaphore()
    for target in targets:
        pl.semaphore_signal(barrier, inc=1, device_id=target, device_id_type=MESH)

    mine = place * 2 + x
    loads = (
        pltpu.make_async_copy(a_in, held_a.at[mine, 0:rows, :], own_sems.at[0]),
        pltpu.make_async_copy(b_in, held_b.at[mine], own_sems.at[1]),
        pltpu.make_async_copy(labels_in, labels_held, own_sems.at[2]),
        pltpu.make_async_copy(plan_in, plan, own_sems.at[3]),
    )
    for load in loads:
        load.start()
    for load in loads:
        load.wait()
    labels = labels_held[...]
    high = lax.shift_right_logical(labels, 8).astype(jnp.float32)
    low = jnp.bitwise_and(labels, 255).astype(jnp.float32)
    line = lax.broadcasted_iota(jnp.int32, (EXTRA, rows), 0)
    coded = jnp.where(line == 0, high, jnp.where(line == 1, low, 0.0))
    held_a[mine, rows : rows + EXTRA, :] = coded.astype(jnp.bfloat16)
    pl.semaphore_wait(barrier, 4)
    send_own_first(start)
    start(0, 0, place, CROSS)
    own_to_mate = (
        to_mate(held_a.at[mine], mate_a, 0),
        to_mate(held_b.at[mine], mate_b, 1),
    )
    for each in own_to_mate:
        each.start()

    def decode(code):
        code = code.astype(jnp.float32)
        return code[0:1] * 256.0 + code[1:2]

    column = lax.broadcasted_iota(jnp.int32, (rows, rows), 1).astype(jnp.float32)

    missing = sum(range(4)) - group
    for slot in range(plan.shape[0]):
        missing -= plan[slot, group]
    swap_1 = missing == across
    swap_2 = missing == 3 - group
    swaps = (None, swap_1, swap_2)

    def pick(swap, one, other):
        return lax.select(jnp.broadcast_to(swap, one.shape), one, other)

    def scale(block):
        return (block.astype(jnp.float32) * (0.5 * factor)).astype(jnp.bfloat16)

    def spread(marks):
        return jnp.transpose(jnp.broadcast_to(marks, (rows, rows))) - column

    def part_of(index):
        return slice(index * rows, (index + 1) * rows)

    scaled_a[part_of(0)] = scale(held_a[mine, 0:rows, :])
    scaled_b[part_of(0)] = scale(held_b[mine])
    offsets[part_of(0)] = spread(labels.astype(jnp.float32))
    total_a[...] = jnp.zeros_like(total_a)
    total_b[...] = jnp.zeros_like(total_b)

    send_own_first(sent)
    send_own_then(start)
    arrived(0, 1, place)
    send_crossed(start)
    for each in own_to_mate:
        each.wait_recv()
    scaled_a[part_of(2)] = scale(mate_a[0:rows, :])
    scaled_b[part_of(2)] = scale(mate_b[...])
    offsets[part_of(2)] = spread(decode(mate_a[rows : rows + EXTRA, :]))
    for ref in (scaled_a, scaled_b, offsets):
        ref[part_of(1)] = pick(swap_1, ref[part_of(2)], ref[part_of(0)])

    owners = (group, jnp.where(swap_1, mate, group), mate)
    others = (group, jnp.where(swap_1, group, across), jnp.where(swap_2, group, across))
    own_firsts = [((one * n + member) * rows).astype(jnp.float32) for one in owners]

    def work(spot):
        base = spot * 2
        at = member_at(spot) * rows
        row = lax.broadcasted_iota(jnp.int32, (rows, rows), 0).astype(jnp.float32)
        near, far = base + x, base + 1 - x
        near_keys, far_keys = held_b[near], held_b[far]
        near_queries, far_queries = held_a[near, 0:rows, :], held_a[far, 0:rows, :]
        near_marks = decode(held_a[near, rows : rows + EXTRA, :])
        far_marks = decode(held_a[far, rows : rows + EXTRA, :])
        for index in range(3):
            part = part_of(index)
            keys, queries, marks = near_keys, near_queries, near_marks
            if index > 0:
                keys = pick(swaps[index], near_keys, far_keys)
                queries = pick(swaps[index], near_queries, far_queries)
                marks = pick(swaps[index], near_marks, far_marks)
            first = (others[index] * n * rows + at).astype(jnp.float32)
            twice = jnp.tanh(dot_rows(scaled_a[part], keys) + 0.5 * logit_bias)
            twice += jnp.where(offsets[part] == first, -1.0, 1.0)
            total_a[part] += jnp.dot(
                twice.astype(jnp.bfloat16), keys, preferred_element_type=jnp.float32
            )
            twice = jnp.tanh(dot_rows(scaled_b[part], queries) + 0.5 * logit_bias)
            twice += jnp.where(marks - own_firsts[index] == row, -1.0, 1.0)
            total_b[part] += jnp.dot(
                twice.astype(jnp.bfloat16), queries, preferred_element_type=jnp.float32
            )

    def step_body(step, carry):
        last = step - 1
        count = jnp.where(jnp.logical_or(last == 0, last == half), 1, 2)

        def turn(index, carry):
            spot = lax.rem(place + n + (2 * index - 1) * last, n)
            arrived(1, 1, spot)
            work(spot)

            @pl.when(index == 0)
            def _():
                send_a_behind(0, step, start, arrived)
                send_a_ahead(0, step, start, arrived)
                send_b_behind(2 * step, start, arrived)
                send_b_ahead(2 * step, start, arrived)

            return carry

        send_b_behind(2 * step - 1, start, arrived)
        send_b_ahead(2 * step - 1, start, arrived)
        lax.fori_loop(0, count, turn, 0)
        send_a_behind(1, step, start, arrived)
        send_a_ahead(1, step, start, arrived)
        return carry

    lax.fori_loop(1, half + 2, step_body, 0)

    shares = (
        to_mate(total_a.at[2 * rows : 3 * rows], share_a, 2),
        to_mate(total_b.at[2 * rows : 3 * rows], share_b, 3),
    )
    stores = (
        pltpu.make_async_copy(total_a.at[0:rows], own_a, own_sems.at[0]),
        pltpu.make_async_copy(total_b.at[0:rows], own_b, own_sems.at[1]),
    )
    for total, share, store in zip((total_a, total_b), shares, stores):
        middle = total[part_of(1)]
        nothing = jnp.zeros_like(middle)
        total[part_of(2)] += pick(swap_1, middle, nothing)
        share.start()
        total[part_of(0)] += pick(swap_1, nothing, middle)
        store.start()

    sent(0, 0, place, CROSS)
    send_own_then(sent)
    send_crossed(sent)
    for each in own_to_mate:
        each.wait_send()

    def drain_body(step, carry):
        send_b_behind(step, sent)
        send_b_ahead(step, sent)
        for q in range(2):
            send_a_behind(q, step, sent)
            send_a_ahead(q, step, sent)
        return carry

    lax.fori_loop(1, half + 1, drain_body, 0)

    for store in stores:
        store.wait()
    for share in shares:
        share.wait_recv()
        share.wait_send()


def finish(factor, own_a, own_b, share_a, share_b, out_a, out_b):
    out_a[...] = (own_a[...] + share_a[...]) * (0.5 * factor)
    out_b[...] = (own_b[...] + share_b[...]) * (0.5 * factor)


def shards(views_a, views_b, positives, plan):
    rows, width = views_a.shape
    n = lax.axis_size("dev")
    slots = 2 * n
    factor = logit_scale / math.sqrt(width)
    vmem, hbm = (pl.BlockSpec(memory_space=space) for space in (pltpu.VMEM, pl.ANY))
    out = jax.ShapeDtypeStruct((rows, width), jnp.float32)
    sums = pl.pallas_call(
        functools.partial(kernel, n, factor),
        out_shape=(out,) * 4,
        in_specs=[hbm] * 4,
        out_specs=(hbm,) * 4,
        scratch_shapes=[
            pltpu.VMEM((slots, rows + EXTRA, width), jnp.bfloat16),
            pltpu.VMEM((slots, rows, width), jnp.bfloat16),
            pltpu.VMEM((rows + EXTRA, width), jnp.bfloat16),
            pltpu.VMEM((rows, width), jnp.bfloat16),
            pltpu.VMEM((3 * rows, width), jnp.float32),
            pltpu.VMEM((3 * rows, width), jnp.float32),
            pltpu.VMEM((3 * rows, width), jnp.bfloat16),
            pltpu.VMEM((3 * rows, width), jnp.bfloat16),
            pltpu.VMEM((3 * rows, rows), jnp.float32),
            pltpu.VMEM((1, rows), jnp.int32),
            pltpu.SMEM(plan.shape, jnp.int32),
            pltpu.SemaphoreType.DMA((4,)),
            pltpu.SemaphoreType.DMA((slots,)),
            pltpu.SemaphoreType.DMA((slots,)),
            pltpu.SemaphoreType.DMA((3, slots)),
            pltpu.SemaphoreType.DMA((3, slots)),
            pltpu.SemaphoreType.DMA((4,)),
            pltpu.SemaphoreType.DMA((4,)),
        ],
        compiler_params=pltpu.CompilerParams(
            collective_id=0, has_side_effects=True, vmem_limit_bytes=60 << 20
        ),
        cost_estimate=pl.CostEstimate(
            flops=12 * slots * rows * rows * width,
            bytes_accessed=4 * rows * width * 4,
            transcendentals=3 * slots * rows * rows,
        ),
    )(views_a, views_b, positives.reshape(1, rows), plan)
    return pl.pallas_call(
        functools.partial(finish, factor),
        out_shape=(out, out),
        in_specs=[vmem] * 4,
        out_specs=(vmem, vmem),
        compiler_params=pltpu.CompilerParams(vmem_limit_bytes=60 << 20),
    )(*sums)


def solution(mesh):
    placed = (P(("grp", "dev"), None), P(("grp", "dev"), None), P(("grp", "dev")), P())
    return jax.shard_map(
        shards,
        mesh=mesh,
        in_specs=placed,
        out_specs=(P(("grp", "dev"), None), P(("grp", "dev"), None)),
        check_vma=False,
    )
```

```python
import functools
import math

import jax
import jax.numpy as jnp
from jax import lax
from jax.experimental import pallas as pl
from jax.experimental.pallas import tpu as pltpu
from jax.sharding import PartitionSpec as P

logit_scale = 2.0
logit_bias = -6.0

MESH = pl.DeviceIdType.MESH
RIGHT, LEFT, CROSS, SIBLING = range(4)
EXTRA = 16


def dot_rows(left, right):
    return lax.dot_general(left, right, (((1,), (1,)), ((), ())), preferred_element_type=jnp.float32)


def kernel(
    n, factor, a_in, b_in, labels_in, plan_in, own_a, own_b, share_a, share_b,
    held_a, held_b, mate_a, mate_b, total_a, total_b,
    scaled_a, scaled_b, offsets, labels_held, plan,
    own_sems, recv_a, recv_b, send_a, send_b, mate_send, mate_recv,
):
    rows, width = a_in.shape
    half = n // 2
    group, member = lax.axis_index("grp"), lax.axis_index("dev")
    x, core = lax.div(group, 2), lax.rem(group, 2)
    across, mate = (1 - x) * 2 + core, x * 2 + 1 - core

    odd, pair = lax.rem(member, 2), lax.div(member, 2)
    place = (1 - odd) * pair + odd * (n - 1 - pair)

    def member_at(spot):
        back = lax.div(spot, half)
        return (1 - back) * 2 * spot + back * (2 * (n - 1 - spot) + 1)

    targets = (
        (group, member_at(lax.rem(place + 1, n))),
        (group, member_at(lax.rem(place + n - 1, n))),
        (across, member),
        (mate, member),
    )

    def behind(step):
        return lax.rem(place + n - step, n)

    def ahead(step):
        return lax.rem(place + step, n)

    def copy(side, q, spot, kind):
        held, recv, send = ((held_a, recv_a, send_a), (held_b, recv_b, send_b))[side]
        slot = spot * 2 + (x if q == 0 else 1 - x)
        return pltpu.make_async_remote_copy(
            src_ref=held.at[slot],
            dst_ref=held.at[slot],
            send_sem=send.at[kind, q * n + spot],
            recv_sem=recv.at[slot],
            device_id=targets[kind],
            device_id_type=MESH,
        )

    def arrived(side, q, spot):
        copy(side, q, spot, CROSS).wait_recv()

    def start(side, q, spot, kind):
        copy(side, q, spot, kind).start()

    def sent(side, q, spot, kind):
        copy(side, q, spot, kind).wait_send()

    def send_b_behind(step, act, first=None):
        @pl.when(step < half)
        def _():
            spot = behind(step)
            if first is not None:
                first(1, 0, spot)

            @pl.when(step < half - 1)
            def _():
                act(1, 0, spot, RIGHT)

            act(1, 0, spot, CROSS)

    def send_b_ahead(step, act, first=None):
        @pl.when(step <= half)
        def _():
            spot = ahead(step)
            if first is not None:
                first(1, 0, spot)

            @pl.when(step < half)
            def _():
                act(1, 0, spot, LEFT)

            act(1, 0, spot, CROSS)

    def send_a_behind(q, step, act, first=None):
        farthest = half - q

        @pl.when(step <= farthest)
        def _():
            spot = behind(step)
            if first is not None:
                first(0, q, spot)

            @pl.when(step < farthest)
            def _():
                act(0, q, spot, RIGHT)

            if q == 0 and half == 1:
                act(0, q, spot, CROSS)

    def send_a_ahead(q, step, act, first=None):
        farthest = half - 1 + q

        @pl.when(step <= farthest)
        def _():
            spot = ahead(step)
            if first is not None:
                first(0, q, spot)

            @pl.when(step < farthest)
            def _():
                act(0, q, spot, LEFT)

            if q == 0:

                @pl.when(step == 1)
                def _():
                    act(0, q, spot, CROSS)

    def send_own(act):
        act(1, 0, place, LEFT)
        if half > 1:
            act(1, 0, place, RIGHT)
        act(0, 0, place, CROSS)
        act(0, 0, place, RIGHT)
        if half > 1:
            act(0, 0, place, LEFT)
        act(1, 0, place, CROSS)

    def send_crossed(act):
        if half > 1:
            act(0, 1, place, RIGHT)

    def to_mate(source, target, index):
        return pltpu.make_async_remote_copy(
            src_ref=source,
            dst_ref=target,
            send_sem=mate_send.at[index],
            recv_sem=mate_recv.at[index],
            device_id=targets[SIBLING],
            device_id_type=MESH,
        )

    barrier = pltpu.get_barrier_semaphore()
    for target in targets:
        pl.semaphore_signal(barrier, inc=1, device_id=target, device_id_type=MESH)

    mine = place * 2 + x
    loads = (
        pltpu.make_async_copy(a_in, held_a.at[mine, 0:rows, :], own_sems.at[0]),
        pltpu.make_async_copy(b_in, held_b.at[mine], own_sems.at[1]),
        pltpu.make_async_copy(labels_in, labels_held, own_sems.at[2]),
        pltpu.make_async_copy(plan_in, plan, own_sems.at[3]),
    )
    for load in loads:
        load.start()
    for load in loads:
        load.wait()
    labels = labels_held[...]
    high = lax.shift_right_logical(labels, 8).astype(jnp.float32)
    low = jnp.bitwise_and(labels, 255).astype(jnp.float32)
    line = lax.broadcasted_iota(jnp.int32, (EXTRA, rows), 0)
    coded = jnp.where(line == 0, high, jnp.where(line == 1, low, 0.0))
    held_a[mine, rows : rows + EXTRA, :] = coded.astype(jnp.bfloat16)
    pl.semaphore_wait(barrier, 4)
    send_own(start)
    own_to_mate = (
        to_mate(held_a.at[mine], mate_a, 0),
        to_mate(held_b.at[mine], mate_b, 1),
    )
    for each in own_to_mate:
        each.start()

    def decode(code):
        code = code.astype(jnp.float32)
        return code[0:1] * 256.0 + code[1:2]

    column = lax.broadcasted_iota(jnp.int32, (rows, rows), 1).astype(jnp.float32)

    missing = sum(range(4)) - group
    for slot in range(plan.shape[0]):
        missing -= plan[slot, group]
    swap_1 = missing == across
    swap_2 = missing == 3 - group
    swaps = (None, swap_1, swap_2)

    def pick(swap, one, other):
        return lax.select(jnp.broadcast_to(swap, one.shape), one, other)

    def scale(block):
        return (block.astype(jnp.float32) * (0.5 * factor)).astype(jnp.bfloat16)

    def spread(marks):
        return jnp.transpose(jnp.broadcast_to(marks, (rows, rows))) - column

    def part_of(index):
        return slice(index * rows, (index + 1) * rows)

    scaled_a[part_of(0)] = scale(held_a[mine, 0:rows, :])
    scaled_b[part_of(0)] = scale(held_b[mine])
    offsets[part_of(0)] = spread(labels.astype(jnp.float32))
    total_a[...] = jnp.zeros_like(total_a)
    total_b[...] = jnp.zeros_like(total_b)

    arrived(0, 1, place)
    send_crossed(start)
    for each in own_to_mate:
        each.wait_recv()
    scaled_a[part_of(2)] = scale(mate_a[0:rows, :])
    scaled_b[part_of(2)] = scale(mate_b[...])
    offsets[part_of(2)] = spread(decode(mate_a[rows : rows + EXTRA, :]))
    for ref in (scaled_a, scaled_b, offsets):
        ref[part_of(1)] = pick(swap_1, ref[part_of(2)], ref[part_of(0)])

    owners = (group, jnp.where(swap_1, mate, group), mate)
    others = (group, jnp.where(swap_1, group, across), jnp.where(swap_2, group, across))
    own_firsts = [((one * n + member) * rows).astype(jnp.float32) for one in owners]

    def work(spot):
        base = spot * 2
        at = member_at(spot) * rows
        row = lax.broadcasted_iota(jnp.int32, (rows, rows), 0).astype(jnp.float32)
        near, far = base + x, base + 1 - x
        near_keys, far_keys = held_b[near], held_b[far]
        near_queries, far_queries = held_a[near, 0:rows, :], held_a[far, 0:rows, :]
        near_marks = decode(held_a[near, rows : rows + EXTRA, :])
        far_marks = decode(held_a[far, rows : rows + EXTRA, :])
        for index in range(3):
            part = part_of(index)
            keys, queries, marks = near_keys, near_queries, near_marks
            if index > 0:
                keys = pick(swaps[index], near_keys, far_keys)
                queries = pick(swaps[index], near_queries, far_queries)
                marks = pick(swaps[index], near_marks, far_marks)
            first = (others[index] * n * rows + at).astype(jnp.float32)
            twice = jnp.tanh(dot_rows(scaled_a[part], keys) + 0.5 * logit_bias)
            twice += jnp.where(offsets[part] == first, -1.0, 1.0)
            total_a[part] += jnp.dot(
                twice.astype(jnp.bfloat16), keys, preferred_element_type=jnp.float32
            )
            twice = jnp.tanh(dot_rows(scaled_b[part], queries) + 0.5 * logit_bias)
            twice += jnp.where(marks - own_firsts[index] == row, -1.0, 1.0)
            total_b[part] += jnp.dot(
                twice.astype(jnp.bfloat16), queries, preferred_element_type=jnp.float32
            )

    def step_body(step, carry):
        last = step - 1
        count = jnp.where(jnp.logical_or(last == 0, last == half), 1, 2)

        def turn(index, carry):
            spot = lax.rem(place + n + (2 * index - 1) * last, n)
            arrived(1, 1, spot)
            work(spot)

            @pl.when(index == 0)
            def _():
                send_a_behind(0, step, start, arrived)
                send_a_ahead(0, step, start, arrived)
                send_b_behind(2 * step, start, arrived)
                send_b_ahead(2 * step, start, arrived)

                @pl.when(step < half)
                def _():
                    send_a_behind(1, step, start, arrived)
                    send_a_ahead(1, step, start, arrived)

            return carry

        send_b_behind(2 * step - 1, start, arrived)
        send_b_ahead(2 * step - 1, start, arrived)
        lax.fori_loop(0, count, turn, 0)

        @pl.when(step == half)
        def _():
            send_a_behind(1, step, start, arrived)
            send_a_ahead(1, step, start, arrived)

        return carry

    lax.fori_loop(1, half + 2, step_body, 0)

    shares = (
        to_mate(total_a.at[2 * rows : 3 * rows], share_a, 2),
        to_mate(total_b.at[2 * rows : 3 * rows], share_b, 3),
    )
    stores = (
        pltpu.make_async_copy(total_a.at[0:rows], own_a, own_sems.at[0]),
        pltpu.make_async_copy(total_b.at[0:rows], own_b, own_sems.at[1]),
    )
    for total, share, store in zip((total_a, total_b), shares, stores):
        middle = total[part_of(1)]
        nothing = jnp.zeros_like(middle)
        total[part_of(2)] += pick(swap_1, middle, nothing)
        share.start()
        total[part_of(0)] += pick(swap_1, nothing, middle)
        store.start()

    send_own(sent)
    send_crossed(sent)
    for each in own_to_mate:
        each.wait_send()

    def drain_body(step, carry):
        send_b_behind(step, sent)
        send_b_ahead(step, sent)
        for q in range(2):
            send_a_behind(q, step, sent)
            send_a_ahead(q, step, sent)
        return carry

    lax.fori_loop(1, half + 1, drain_body, 0)

    for store in stores:
        store.wait()
    for share in shares:
        share.wait_recv()
        share.wait_send()


def finish(factor, own_a, own_b, share_a, share_b, out_a, out_b):
    out_a[...] = (own_a[...] + share_a[...]) * (0.5 * factor)
    out_b[...] = (own_b[...] + share_b[...]) * (0.5 * factor)


def shards(views_a, views_b, positives, plan):
    rows, width = views_a.shape
    n = lax.axis_size("dev")
    slots = 2 * n
    factor = logit_scale / math.sqrt(width)
    vmem, hbm = (pl.BlockSpec(memory_space=space) for space in (pltpu.VMEM, pl.ANY))
    out = jax.ShapeDtypeStruct((rows, width), jnp.float32)
    sums = pl.pallas_call(
        functools.partial(kernel, n, factor),
        out_shape=(out,) * 4,
        in_specs=[hbm] * 4,
        out_specs=(hbm,) * 4,
        scratch_shapes=[
            pltpu.VMEM((slots, rows + EXTRA, width), jnp.bfloat16),
            pltpu.VMEM((slots, rows, width), jnp.bfloat16),
            pltpu.VMEM((rows + EXTRA, width), jnp.bfloat16),
            pltpu.VMEM((rows, width), jnp.bfloat16),
            pltpu.VMEM((3 * rows, width), jnp.float32),
            pltpu.VMEM((3 * rows, width), jnp.float32),
            pltpu.VMEM((3 * rows, width), jnp.bfloat16),
            pltpu.VMEM((3 * rows, width), jnp.bfloat16),
            pltpu.VMEM((3 * rows, rows), jnp.float32),
            pltpu.VMEM((1, rows), jnp.int32),
            pltpu.SMEM(plan.shape, jnp.int32),
            pltpu.SemaphoreType.DMA((4,)),
            pltpu.SemaphoreType.DMA((slots,)),
            pltpu.SemaphoreType.DMA((slots,)),
            pltpu.SemaphoreType.DMA((3, slots)),
            pltpu.SemaphoreType.DMA((3, slots)),
            pltpu.SemaphoreType.DMA((4,)),
            pltpu.SemaphoreType.DMA((4,)),
        ],
        compiler_params=pltpu.CompilerParams(
            collective_id=0, has_side_effects=True, vmem_limit_bytes=60 << 20
        ),
        cost_estimate=pl.CostEstimate(
            flops=12 * slots * rows * rows * width,
            bytes_accessed=4 * rows * width * 4,
            transcendentals=3 * slots * rows * rows,
        ),
    )(views_a, views_b, positives.reshape(1, rows), plan)
    return pl.pallas_call(
        functools.partial(finish, factor),
        out_shape=(out, out),
        in_specs=[vmem] * 4,
        out_specs=(vmem, vmem),
        compiler_params=pltpu.CompilerParams(vmem_limit_bytes=60 << 20),
    )(*sums)


def solution(mesh):
    placed = (P(("grp", "dev"), None), P(("grp", "dev"), None), P(("grp", "dev")), P())
    return jax.shard_map(
        shards,
        mesh=mesh,
        in_specs=placed,
        out_specs=(P(("grp", "dev"), None), P(("grp", "dev"), None)),
        check_vma=False,
    )
```
